256 devices in a mesh: member: 16 (over x_lo, z), shard: 16 (over x_hi, y, core).
Axes of the slice: x: 4 (x_hi: 2, x_lo: 2; x = x_hi * 2 + x_lo), y: 4, z: 8, core: 2. Of those that a mesh axis runs over, the one named last changes fastest.
Arguments:
- tokens: bfloat16 [65536, 4096], P(('member', 'shard')), may hold values from -24 to 24
- cotangent: bfloat16 [65536, 1024], P(('member', 'shard')), may hold values from -6 to 6
- slow_weight: bfloat16 [4096, 1024], P('shard'), may hold values from -0.09375 to 0.09375
- in_scale: float32 [16, 4096], P('member'), may hold values from 0.1 to 1.9
- out_scale: float32 [16, 1024], P('member'), may hold values from 0.1 to 1.9
Outputs:
- outputs: bfloat16 [65536, 1024], P(('member', 'shard'))
- grad_tokens: bfloat16 [65536, 4096], P(('member', 'shard'))
- grad_weight: float32 [4096, 1024], P('shard')
- grad_in_scale: float32 [16, 4096], P('member')
- grad_out_scale: float32 [16, 1024], P('member')
The draws below stay inside these ranges and needn't reach their ends.
All inputs are finite; a program needn't handle non-finite values.
Results may differ from the reference program's by a relative error of at most 0.005.
Values may be sent and summed in bfloat16 or wider, within the bound.
No kernel may reach another device: no remote copies, remote signals or barrier semaphores. Data moves between devices by JAX's collectives and lax.ppermute only.
A program may use at most 128 MiB of HBM per device.

```python
import jax
import jax.numpy as jnp
from jax import lax

D = 4096
E = 1024
MEMBERS = 16
TOKENS = 65536


def strengthened(entries, rng, source, target, parts, factor):
    def block_of(dim):
        return (jnp.arange(entries.shape[dim]) // (entries.shape[dim] // parts)).reshape((-1,) + (1,) * (entries.ndim - 1 - dim))

    near = jax.random.permutation(rng, parts)[block_of(target)]
    far = (block_of(target) + parts // 2) % parts
    return jnp.where((block_of(source) == near) | (block_of(source) == far), factor * entries, entries)


def levels(stream_key, extent, split, smallest, top_value):
    level = 1.0
    for dim, shards_of in split:
        heights = jax.random.uniform(jax.random.fold_in(jax.random.fold_in(stream_key, 6), dim), (shards_of,), jnp.float32, smallest / len(split), top_value / len(split))
        level = level * jnp.repeat(jnp.exp(heights), extent[dim] // shards_of).reshape((-1,) + (1,) * (len(extent) - 1 - dim))
    return level


def normal_values(stream_key, shape, width, reach, shards=(), held_as=jnp.bfloat16):
    values = jax.random.normal(stream_key, shape, jnp.float32) * width
    if len(shards) > 0:
        values = levels(stream_key, shape, shards, -0.22, 0.18) * values
    return jnp.clip(values, min=-reach, max=reach).astype(held_as)


def noise_with(rng, extent, deviation, limit, shards, heavy, kind=jnp.bfloat16):
    entries = deviation * jax.random.normal(rng, extent, jnp.float32)
    if shards:
        entries = entries * levels(rng, extent, shards, -0.22, 0.18)
    return jnp.clip(strengthened(entries, jax.random.fold_in(rng, 3), *heavy), -limit, limit).astype(kind)


def setup_inputs(seed: int = 0) -> dict:
    seeds = jax.random.split(jax.random.key(seed), 6)
    tokens = noise_with(seeds[0], (TOKENS, D), 1.0, 24.0, ((0, 256),), (0, 1, 256, 6.0))
    cotangent = normal_values(seeds[1], (TOKENS, E), 1.0, 6.0, ((0, 256),))
    slow_weight = normal_values(seeds[2], (D, E), D ** -0.5, 0.09375, ((0, 16),))
    in_scale = jnp.clip(1.0 + 0.18 * jax.random.normal(seeds[3], (MEMBERS, D), jnp.float32), 0.1, 1.9)
    out_scale = jnp.clip(1.0 + 0.18 * jax.random.normal(seeds[4], (MEMBERS, E), jnp.float32), 0.1, 1.9)
    return {"tokens": tokens, "cotangent": cotangent, "slow_weight": slow_weight, "in_scale": in_scale, "out_scale": out_scale}


def reference(tokens, cotangent, slow_weight, in_scale, out_scale):
    per_member = TOKENS // MEMBERS
    token_blocks = tokens.reshape(MEMBERS, per_member, D)
    grad_blocks = cotangent.reshape(MEMBERS, per_member, E)

    def member_step(total, item):
        inputs, grads, scale_in, scale_out = item
        scaled = (inputs.astype(jnp.float32) * scale_in).astype(jnp.bfloat16)
        pre_out = jnp.dot(scaled, slow_weight, preferred_element_type=jnp.float32)
        result = (pre_out * scale_out).astype(jnp.bfloat16)
        scaled_grad = (grads.astype(jnp.float32) * scale_out).astype(jnp.bfloat16)
        back = lax.dot_general(scaled_grad, slow_weight, (((1,), (1,)), ((), ())), preferred_element_type=jnp.float32)
        grad_in = (back * scale_in).astype(jnp.bfloat16)
        in_sum = jnp.sum(inputs.astype(jnp.float32) * back, axis=0)
        out_sum = jnp.sum(grads.astype(jnp.float32) * pre_out, axis=0)
        weight_term = lax.dot_general(scaled, scaled_grad, (((0,), (0,)), ((), ())), preferred_element_type=jnp.float32)
        return total + weight_term, (result, grad_in, in_sum, out_sum)

    start = jnp.zeros((D, E), jnp.float32)
    grad_weight, (result, grad_in, in_sum, out_sum) = lax.scan(member_step, start, (token_blocks, grad_blocks, in_scale, out_scale))
    member_norm = 1.0 / (float(per_member) ** 0.5)
    total_norm = 1.0 / (float(TOKENS) ** 0.5)
    return (result.reshape(TOKENS, E), grad_in.reshape(TOKENS, D), grad_weight * total_norm, in_sum * member_norm, out_sum * member_norm)
```

```python
import jax
import jax.numpy as jnp
from jax import lax
from jax.sharding import Mesh, PartitionSpec as P

F32, BF16 = jnp.float32, jnp.bfloat16
XL, Z, XH, Y, C = "xl", "z", "xh", "y", "c"


def ring(size, step):
    return [(i, (i + step) % size) for i in range(size)]


def send_y(a, step):
    return lax.ppermute(a, Y, ring(4, step))


def send_z(a, step):
    return lax.ppermute(a, Z, ring(8, step))


def x_index(place):
    return (place % 2) * 2 + place // 2


def send_x(a, step):
    return lax.ppermute(a, (XL, XH), [(x_index(i), x_index((i + step) % 4)) for i in range(4)])


def x_pairs(a, other):
    return lax.ppermute(a, (XL, XH), [(x_index(i), x_index(other(i))) for i in range(4)])


def swap_core(a):
    return lax.ppermute(a, C, [(0, 1), (1, 0)])


def pick(a, at, axis):
    return lax.dynamic_index_in_dim(a, at, axis, keepdims=False)


def gather_weight(own):
    far = x_pairs(own, lambda i: 3 - i)
    rows = []
    up, down = send_y(own, 1), send_y(own, -1)
    far_up, far_down = send_y(far, 1), send_y(far, -1)
    half = own.shape[0] // 2
    two = jnp.concatenate([send_y(up[:half], 1), send_y(down[half:], -1)], axis=0)
    far_two = jnp.concatenate([send_y(far_up[:half], 1), send_y(far_down[half:], -1)], axis=0)
    return [[own, down, two, up], [far, far_down, far_two, far_up]]


def on_device(tokens, cotangent, slow_weight, in_scale, out_scale):
    xl, z, xh, y, c = (lax.axis_index(a) for a in (XL, Z, XH, Y, C))
    x = 2 * xh + xl
    rows, depth = tokens.shape
    width = cotangent.shape[1]
    piece = depth // 16
    member_norm = 1.0 / float(rows * 16) ** 0.5
    total_norm = 1.0 / float(rows * 256) ** 0.5

    by_slice = tokens.reshape(rows, 8, 2, piece)
    even, odd = by_slice[:, :, 0].reshape(rows, depth // 2), by_slice[:, :, 1].reshape(rows, depth // 2)
    mine = jnp.where(c == 0, even, odd)
    others = swap_core(jnp.where(c == 0, odd, even))
    cot_other = swap_core(cotangent)
    tok = jnp.concatenate([mine, others], axis=0)
    cot = jnp.concatenate([cotangent, cot_other], axis=0).astype(F32)
    scale_slices = in_scale.reshape(8, 2, piece)
    scale = pick(scale_slices, c, 1).reshape(1, depth // 2)
    scaled = (tok.astype(F32) * scale).astype(BF16)
    scaled_grad = (cot * out_scale).astype(BF16)

    gathered = gather_weight(slow_weight)

    part = lax.dot_general(scaled, scaled_grad, (((0,), (0,)), ((), ())), preferred_element_type=F32)
    part = part.reshape(2, 4, 2, piece // 2, width)
    half = width // 2

    a_part = part[..., :half]
    a_sum = pick(a_part, y, 1)
    for step in (1, -1, 2):
        a_sum = a_sum + send_y(pick(a_part, (y + step) % 4, 1).astype(BF16), step).astype(F32)

    b_part = part[..., half:].transpose(0, 2, 1, 3, 4).reshape(4, 4, piece // 2, half)
    b_sum = pick(b_part, x, 0)
    for step in (1, -1, 2):
        b_sum = b_sum + send_x(pick(b_part, (x + step) % 4, 0).astype(BF16), step).astype(F32)

    a_sum = a_sum.reshape(4, piece // 2, half)
    a_last = pick(a_sum, x, 0)
    for step in (1, -1, 2):
        a_last = a_last + send_x(pick(a_sum, (x + step) % 4, 0).astype(BF16), step).astype(F32)
    b_last = pick(b_sum, y, 0)
    for step in (1, -1, 2):
        b_last = b_last + send_y(pick(b_sum, (y + step) % 4, 0).astype(BF16), step).astype(F32)

    both = jnp.concatenate([a_last, b_last], axis=1).reshape(8, piece // 16, width)
    z_sum = pick(both, z, 0)
    for step in (1, -1, 2, -2, 3, -3, 4):
        z_sum = z_sum + send_z(pick(both, (z + step) % 8, 0).astype(BF16), step).astype(F32)
    z_own = z_sum.astype(BF16)
    arrived = {0: z_own}
    for step in (1, -1, 2, -2, 3, -3, 4):
        arrived[(-step) % 8] = send_z(z_own, step)
    rel = jnp.concatenate([arrived[i % 8] for i in range(16)], axis=0)
    half_rows = lax.dynamic_slice_in_dim(rel, (8 - z) * (piece // 16), piece // 2, 0)
    twin = x_pairs(half_rows, lambda i: i ^ 1)
    low = jnp.where(xl == 0, half_rows, twin)
    high = jnp.where(xl == 0, twin, half_rows)
    grad_weight = jnp.concatenate([low, high], axis=0).astype(F32) * total_norm

    weight = jnp.zeros((2, 4, piece, width), BF16)
    for dxh in range(2):
        for dy in range(4):
            weight = lax.dynamic_update_slice(
                weight, gathered[dxh][dy][None, None], (xh ^ dxh, (y + dy) % 4, 0, 0)
            )
    weight = weight.reshape(depth // 2, width)
    pre = jnp.dot(scaled, weight, preferred_element_type=F32)
    back = lax.dot_general(scaled_grad, weight, (((1,), (1,)), ((), ())), preferred_element_type=F32)
    grad_in = (back * scale).astype(BF16)
    pre_own = pre[:rows] + swap_core(pre[rows:].astype(BF16)).astype(F32)
    result = (pre_own * out_scale).astype(BF16)
    grad_other = swap_core(grad_in[rows:]).reshape(rows, 8, piece)
    grad_own = grad_in[:rows].reshape(rows, 8, piece)
    grad_tokens = jnp.stack(
        [jnp.where(c == 0, grad_own, grad_other), jnp.where(c == 0, grad_other, grad_own)], axis=2
    ).reshape(rows, depth)
    in_part = jnp.sum(tok.astype(F32) * back, axis=0, keepdims=True)
    out_part = jnp.sum(cot * pre, axis=0, keepdims=True)
    small = jnp.concatenate([in_part.reshape(2, width), out_part], axis=0)
    for flip in (1, 2):
        small = small + lax.ppermute(small, Y, [(i, i ^ flip) for i in range(4)])
    small = small + lax.ppermute(small, XH, [(0, 1), (1, 0)])
    small_other = swap_core(small)
    out_sum = (small[2:] + small_other[2:]) * member_norm
    in_own = small[:2].reshape(8, piece)
    in_other = small_other[:2].reshape(8, piece)
    in_sum = jnp.stack(
        [jnp.where(c == 0, in_own, in_other), jnp.where(c == 0, in_other, in_own)], axis=1
    ).reshape(1, depth) * member_norm
    return result, grad_tokens, grad_weight, in_sum, out_sum


def solution(mesh):
    wide = Mesh(mesh.devices.reshape(2, 8, 2, 4, 2), (XL, Z, XH, Y, C))
    row, member, shard = P((XL, Z, XH, Y, C), None), P((XL, Z), None), P((XH, Y, C), None)
    return jax.shard_map(
        on_device,
        mesh=wide,
        in_specs=(row, row, shard, member, member),
        out_specs=(row, row, shard, member, member),
        check_vma=False,
    )
```

```python
import functools

import jax
import jax.numpy as jnp
from jax import lax
from jax.experimental import pallas as pl
from jax.experimental.pallas import tpu as pltpu
from jax.sharding import Mesh, PartitionSpec as P

F32, BF16 = jnp.float32, jnp.bfloat16
XL, Z, XH, Y, C = "xl", "z", "xh", "y", "c"
ROWS, DEPTH, WIDTH, PIECE = 256, 4096, 1024, 256
HALF, LANE = WIDTH // 2, PIECE // 2
VMEM = pl.BlockSpec(memory_space=pltpu.VMEM)
PARAMS = pltpu.CompilerParams(vmem_limit_bytes=40 * 2**20)


def send_y(a, step):
    return lax.ppermute(a, Y, [(i, (i + step) % 4) for i in range(4)])


def send_z(a, step):
    return lax.ppermute(a, Z, [(i, (i + step) % 8) for i in range(8)])


def x_index(place):
    return (place % 2) * 2 + place // 2


def send_x(a, step):
    return lax.ppermute(a, (XL, XH), [(x_index(i), x_index((i + step) % 4)) for i in range(4)])


def pairs_x(a, other):
    return lax.ppermute(a, (XL, XH), [(x_index(i), x_index(other(i))) for i in range(4)])


def swap_core(a):
    return lax.ppermute(a, C, [(0, 1), (1, 0)])


def slice_of(pos, dxh, dy):
    return ((pos[0] // 2 + dxh) % 2) * 4 + (pos[1] + dy) % 4


def cost(flops, bytes_accessed):
    return pl.CostEstimate(flops=flops, bytes_accessed=bytes_accessed, transcendentals=0)


def copy_body(pos, src, dst):
    dst[...] = src[...]


def other_half(pos, tokens):
    return pl.pallas_call(
        copy_body,
        out_shape=jax.ShapeDtypeStruct((ROWS, DEPTH // 2), BF16),
        grid_spec=pltpu.PrefetchScalarGridSpec(
            num_scalar_prefetch=1,
            grid=(8,),
            in_specs=[pl.BlockSpec((ROWS, PIECE), lambda j, pos: (0, 2 * j + 1 - pos[2]))],
            out_specs=pl.BlockSpec((ROWS, PIECE), lambda j, pos: (0, j)),
        ),
        compiler_params=PARAMS,
        cost_estimate=cost(0, 2**21),
    )(pos, tokens)


def partial_body(pos, tok, tok_other, cot, cot_other, in_scale, out_scale, grad_ref, *outs):
    a_refs, b_refs = outs[:4], outs[4:]
    i = pl.program_id(0)

    @pl.when(i == 0)
    def _():
        grad_ref[:ROWS] = (cot[...].astype(F32) * out_scale[...]).astype(BF16)
        grad_ref[ROWS:] = (cot_other[...].astype(F32) * out_scale[...]).astype(BF16)

    y_at = (pos[1] + i) % 4
    for k in range(4):
        x_at = (pos[0] + k) % 4
        place = (x_at // 2) * 4 + y_at
        wide = pl.ds(pl.multiple_of(((place * 2 + pos[2]) * 2 + x_at % 2) * LANE, LANE), LANE)
        narrow = pl.ds(pl.multiple_of((place * 2 + x_at % 2) * LANE, LANE), LANE)
        scale = in_scale[:, wide]
        first = (tok[:, wide].astype(F32) * scale).astype(BF16)
        second = (tok_other[:, narrow].astype(F32) * scale).astype(BF16)
        dims = (((0,), (0,)), ((), ()))
        part = lax.dot_general(first, grad_ref[:ROWS], dims, preferred_element_type=F32)
        part = part + lax.dot_general(second, grad_ref[ROWS:], dims, preferred_element_type=F32)
        part = part.astype(BF16)
        b_refs[k][0] = part[:, HALF:]
        for m in range(4):
            @pl.when(i == m)
            def _():
                a_refs[m][k] = part[:, :HALF]


def partials(pos, tokens, tok_other, cot, cot_other, in_scale, out_scale):
    whole = lambda shape: pl.BlockSpec(shape, lambda i, pos: (0,) * len(shape))
    block = jax.ShapeDtypeStruct((4, LANE, HALF), BF16)
    outs = pl.pallas_call(
        partial_body,
        out_shape=[jax.ShapeDtypeStruct((2 * ROWS, WIDTH), BF16)] + [block] * 8,
        grid_spec=pltpu.PrefetchScalarGridSpec(
            num_scalar_prefetch=1,
            grid=(4,),
            in_specs=[
                whole((ROWS, DEPTH)), whole((ROWS, DEPTH // 2)), whole((ROWS, WIDTH)),
                whole((ROWS, WIDTH)), whole((1, DEPTH)), whole((1, WIDTH)),
            ],
            out_specs=[whole((2 * ROWS, WIDTH))]
            + [whole((4, LANE, HALF))] * 4
            + [pl.BlockSpec((1, LANE, HALF), lambda i, pos: (i, 0, 0))] * 4,
        ),
        compiler_params=PARAMS,
        cost_estimate=cost(2 * 2 * ROWS * DEPTH // 2 * WIDTH, 9 * 2**20),
    )(pos, tokens, tok_other, cot, cot_other, in_scale, out_scale)
    return outs[0], outs[1:5], outs[5:]


def sum_body(own, r1, r2, r3, keep, s1, s2, s3):
    for k, out in enumerate((keep, s1, s2, s3)):
        total = own[k].astype(F32) + r1[k].astype(F32) + r2[k].astype(F32) + r3[k].astype(F32)
        out[...] = total.astype(out.dtype)


def sum_blocks(own, arrived):
    shape = (LANE, HALF)
    return pl.pallas_call(
        sum_body,
        out_shape=[jax.ShapeDtypeStruct(shape, F32)] + [jax.ShapeDtypeStruct(shape, BF16)] * 3,
        in_specs=[VMEM] * 4,
        out_specs=[VMEM] * 4,
        compiler_params=PARAMS,
        cost_estimate=cost(2**20, 5 * 2**19),
    )(own, *arrived)


def join_body(pos, a0, a1, a2, a3, b0, b1, b2, b3, keep, send):
    count = LANE // 2
    mine = pos[3] % 2
    for out, at in ((keep, mine), (send, 1 - mine)):
        rows = pl.ds(pl.multiple_of(at * count, count), count)
        for side, refs in ((0, (a0, a1, a2, a3)), (1, (b0, b1, b2, b3))):
            total = refs[0][rows]
            for ref in refs[1:]:
                total = total + ref[rows].astype(F32)
            out[:, side * HALF : (side + 1) * HALF] = total.astype(out.dtype)


def join(pos, a, b):
    shape = (LANE // 2, WIDTH)
    return pl.pallas_call(
        join_body,
        out_shape=[jax.ShapeDtypeStruct(shape, F32), jax.ShapeDtypeStruct(shape, BF16)],
        in_specs=[pl.BlockSpec(memory_space=pltpu.SMEM)] + [VMEM] * 8,
        out_specs=[VMEM] * 2,
        compiler_params=PARAMS,
        cost_estimate=cost(2**20, 2**21),
    )(pos, *a, *b)


def place_body(scale, pos, own, by_z, by_x, by_both, out):
    count = LANE // 2
    me = (pos[0] % 2) * 2 + pos[3] % 2
    for flip, ref in enumerate((own, by_z, by_x, by_both)):
        at = (me // 2 + flip // 2) % 2 * 2 + (me + flip) % 2
        out[pl.ds(pl.multiple_of(at * count, count), count)] = ref[...].astype(F32) * scale


def place(pos, blocks, scale):
    return pl.pallas_call(
        functools.partial(place_body, scale),
        out_shape=jax.ShapeDtypeStruct((PIECE, WIDTH), F32),
        in_specs=[pl.BlockSpec(memory_space=pltpu.SMEM)] + [VMEM] * 4,
        out_specs=VMEM,
        compiler_params=PARAMS,
        cost_estimate=cost(2**18, 2**20),
    )(pos, *blocks)


def layer_body(order, last, pos, tok, tok_other, grad, in_scale, cot, cot_other, *refs):
    weights, refs = refs[:4], refs[4:]
    if last:
        (pre_in, small_in, _), refs = refs[:3], refs[3:]
        own_ref, other_ref, pre_ref, pre_other, small, total = refs
    else:
        own_ref, other_ref, pre_ref, small = refs
        total = pre_ref
    i = pl.program_id(0)

    @pl.when(i == 0)
    def _():
        if last:
            total[...] = pre_in[...]
            small[...] = small_in[...]
        else:
            small[...] = jnp.zeros_like(small)

    for m, (dxh, dy) in enumerate(order):
        @pl.when(i == m)
        def _():
            at = slice_of(pos, dxh, dy)
            wide = pl.ds(pl.multiple_of((at * 2 + pos[2]) * PIECE, PIECE), PIECE)
            narrow = pl.ds(pl.multiple_of(at * PIECE, PIECE), PIECE)
            scale = in_scale[:, wide]
            weight = weights[m][...]
            sums = jnp.zeros((1, PIECE), F32)
            for part, values in ((0, tok[:, wide]), (1, tok_other[:, narrow])):
                rows = slice(part * ROWS, (part + 1) * ROWS)
                values = values.astype(F32)
                scaled = (values * scale).astype(BF16)
                pre = jnp.dot(scaled, weight, preferred_element_type=F32)
                if m == 0 and not last:
                    total[rows] = pre
                else:
                    total[rows] += pre
                back = lax.dot_general(
                    grad[rows], weight, (((1,), (1,)), ((), ())), preferred_element_type=F32
                )
                (own_ref, other_ref)[part][...] = (back * scale).astype(BF16)
                sums = sums + jnp.sum(values * back, axis=0, keepdims=True)
            small[:, wide] = sums

    if last:
        @pl.when(i == 3)
        def _():
            pre_ref[...] = total[:ROWS]
            pre_other[...] = total[ROWS:].astype(BF16)
            small[:, DEPTH:] = jnp.sum(
                cot[...].astype(F32) * total[:ROWS] + cot_other[...].astype(F32) * total[ROWS:],
                axis=0, keepdims=True,
            )


def layer(pos, order, tokens, tok_other, grad, in_scale, cot, cot_other, weights, before=None):
    whole = lambda shape: pl.BlockSpec(shape, lambda i, pos: (0,) * len(shape))
    shaped = jax.ShapeDtypeStruct
    dxhs = [o[0] for o in order]
    dys = [o[1] for o in order]

    def column(i, pos):
        dxh, dy = dxhs[3], dys[3]
        for m in range(3):
            dxh = jnp.where(i == m, dxhs[m], dxh)
            dy = jnp.where(i == m, dys[m], dy)
        return 0, slice_of(pos, dxh, dy) * 2 + pos[2]

    in_specs = [
        whole((ROWS, DEPTH)), whole((ROWS, DEPTH // 2)), whole((2 * ROWS, WIDTH)), whole((1, DEPTH)),
        whole((ROWS, WIDTH)), whole((ROWS, WIDTH)),
    ] + [whole((PIECE, WIDTH))] * 4
    operands = [tokens, tok_other, grad, in_scale, cot, cot_other, *weights]
    out_shape = [shaped((ROWS, DEPTH), BF16), shaped((ROWS, DEPTH // 4), BF16)]
    out_specs = [pl.BlockSpec((ROWS, PIECE), column), pl.BlockSpec((ROWS, PIECE), lambda i, pos: (0, i))]
    scratch, aliases = [], {}
    small = shaped((1, DEPTH + WIDTH), F32)
    if before is None:
        out_shape += [shaped((2 * ROWS, WIDTH), F32), small]
        out_specs += [whole((2 * ROWS, WIDTH)), whole(small.shape)]
    else:
        own, pre, sums = before
        operands += [pre, sums, own]
        in_specs += [whole((2 * ROWS, WIDTH)), whole(small.shape), pl.BlockSpec(memory_space=pl.ANY)]
        aliases = {len(operands): 0}
        out_shape += [shaped((ROWS, WIDTH), F32), shaped((ROWS, WIDTH), BF16), small]
        out_specs += [whole((ROWS, WIDTH)), whole((ROWS, WIDTH)), whole(small.shape)]
        scratch = [pltpu.VMEM((2 * ROWS, WIDTH), F32)]
    return pl.pallas_call(
        functools.partial(layer_body, order, before is not None),
        out_shape=out_shape,
        grid_spec=pltpu.PrefetchScalarGridSpec(
            num_scalar_prefetch=1, grid=(4,), in_specs=in_specs, out_specs=out_specs,
            scratch_shapes=scratch,
        ),
        input_output_aliases=aliases,
        compiler_params=PARAMS,
        cost_estimate=cost(2 * 2 * 2 * ROWS * WIDTH * WIDTH, 10 * 2**20),
    )(pos, *operands)


def fill_body(pos, first, second, _, out):
    j = pl.program_id(0)

    @pl.when(j < 4)
    def _():
        out[...] = first[...]

    @pl.when(j >= 4)
    def _():
        out[...] = second[...]


def fill(pos, orders, first, second, own):
    flat = orders[0] + orders[1]

    def column(j, pos):
        dxh, dy = flat[7]
        for m in range(7):
            dxh = jnp.where(j == m, flat[m][0], dxh)
            dy = jnp.where(j == m, flat[m][1], dy)
        return 0, slice_of(pos, dxh, dy) * 2 + 1 - pos[2]

    return pl.pallas_call(
        fill_body,
        out_shape=jax.ShapeDtypeStruct((ROWS, DEPTH), BF16),
        grid_spec=pltpu.PrefetchScalarGridSpec(
            num_scalar_prefetch=1,
            grid=(8,),
            in_specs=[
                pl.BlockSpec((ROWS, PIECE), lambda j, pos: (0, jnp.minimum(j, 3))),
                pl.BlockSpec((ROWS, PIECE), lambda j, pos: (0, jnp.maximum(j, 4) - 4)),
                pl.BlockSpec(memory_space=pl.ANY),
            ],
            out_specs=pl.BlockSpec((ROWS, PIECE), column),
        ),
        input_output_aliases={3: 0},
        compiler_params=PARAMS,
        cost_estimate=cost(0, 2**21),
    )(pos, first, second, own)


def on_device(tokens, cotangent, slow_weight, in_scale, out_scale):
    xl, z, xh, y, c = (lax.axis_index(a) for a in (XL, Z, XH, Y, C))
    pos = jnp.stack([2 * xh + xl, y, c, z]).astype(jnp.int32)
    member_norm = 1.0 / float(ROWS * 16) ** 0.5
    total_norm = 1.0 / float(ROWS * 256) ** 0.5

    cot_other = swap_core(cotangent)
    up, down = send_y(slow_weight, 1), send_y(slow_weight, -1)
    far = pairs_x(slow_weight, lambda i: 3 - i)
    tok_other = swap_core(other_half(pos, tokens))

    grad, a_part, b_part = partials(pos, tokens, tok_other, cotangent, cot_other, in_scale, out_scale)
    far, up, down, a_part, b_part = lax.optimization_barrier((far, up, down, a_part, b_part))

    half = PIECE // 2
    far_up = send_y(jnp.concatenate([far, up[:half]], axis=0), 1)
    far_down = send_y(jnp.concatenate([far, down[half:]], axis=0), -1)
    a_in = [send_y(a_part[1], 1), send_y(a_part[3], -1), send_y(a_part[2], 2)]
    b_in = [send_x(b_part[1], 1), send_x(b_part[3], -1), send_x(b_part[2], 2)]
    orders = ((0, 0), (0, 1), (0, 3), (1, 0)), ((0, 2), (1, 3), (1, 1), (1, 2))
    own, others_1, pre, small = layer(
        pos, orders[0], tokens, tok_other, grad, in_scale, cotangent, cot_other,
        (slow_weight, down, up, far),
    )
    far_two_up = send_y(far_up[:half], 1)
    far_two_down = send_y(far_down[half:PIECE], -1)

    a_own, *a_out = sum_blocks(a_part[0], a_in)
    b_own, *b_out = sum_blocks(b_part[0], b_in)
    b_in = [send_y(b_out[0], 1), send_y(b_out[2], -1), send_y(b_out[1], 2)]
    a_in = [send_x(a_out[0], 1), send_x(a_out[2], -1), send_x(a_out[1], 2)]

    two = jnp.concatenate([far_up[PIECE:], far_down[PIECE:]], axis=0)
    far_two = jnp.concatenate([far_two_up, far_two_down], axis=0)
    own, others_2, pre_own, pre_other, small = layer(
        pos, orders[1], tokens, tok_other, grad, in_scale, cotangent, cot_other,
        (two, far_up[:PIECE], far_down[:PIECE], far_two), (own, pre, small),
    )
    pre_other = swap_core(pre_other)
    small = small + swap_core(small)
    others_1, others_2 = swap_core(others_1), swap_core(others_2)

    keep, out = join(pos, [a_own, *a_in], [b_own, *b_in])
    pair = lambda a: lax.ppermute(a, Z, [(i, i ^ 1) for i in range(8)])
    mine = (keep + pair(out).astype(F32)).astype(BF16)
    plus, minus, across = send_z(mine, 2), send_z(mine, -2), send_z(mine, 4)

    result = ((pre_own + pre_other.astype(F32)) * out_scale).astype(BF16)
    grad_tokens = fill(pos, orders, others_1, others_2, own)
    small = small + send_y(small, 2)
    small = small + lax.ppermute(small, Y, [(i, i ^ 1) for i in range(4)])
    small = small + lax.ppermute(small, XH, [(0, 1), (1, 0)])

    summed = (mine.astype(F32) + across.astype(F32)) + (plus.astype(F32) + minus.astype(F32))
    summed = summed.astype(BF16)
    by_z = pair(summed)
    by_x = pairs_x(summed, lambda i: i ^ 1)
    by_both = lax.ppermute(
        summed, (XL, Z), [(i, i ^ 9) for i in range(16)]
    )
    grad_weight = place(pos, (summed, by_z, by_x, by_both), total_norm)
    small = small * member_norm
    return result, grad_tokens, grad_weight, small[:, :DEPTH], small[:, DEPTH:]


def solution(mesh):
    wide = Mesh(mesh.devices.reshape(2, 8, 2, 4, 2), (XL, Z, XH, Y, C))
    row, member, shard = P((XL, Z, XH, Y, C), None), P((XL, Z), None), P((XH, Y, C), None)
    return jax.shard_map(
        on_device,
        mesh=wide,
        in_specs=(row, row, shard, member, member),
        out_specs=(row, row, shard, member, member),
        check_vma=False,
    )
```

```python
import functools

import jax
import jax.numpy as jnp
from jax import lax
from jax.experimental import pallas as pl
from jax.experimental.pallas import tpu as pltpu
from jax.sharding import Mesh, PartitionSpec as P

F32, BF16 = jnp.float32, jnp.bfloat16
XL, Z, XH, Y, C = "xl", "z", "xh", "y", "c"
ROWS, DEPTH, WIDTH, PIECE = 256, 4096, 1024, 256
HALF, LANE = WIDTH // 2, PIECE // 2
VMEM = pl.BlockSpec(memory_space=pltpu.VMEM)
PARAMS = pltpu.CompilerParams(vmem_limit_bytes=40 * 2**20)


def send_y(a, step):
    return lax.ppermute(a, Y, [(i, (i + step) % 4) for i in range(4)])


def send_z(a, step):
    return lax.ppermute(a, Z, [(i, (i + step) % 8) for i in range(8)])


def x_index(place):
    return (place % 2) * 2 + place // 2


def send_x(a, step):
    return lax.ppermute(a, (XL, XH), [(x_index(i), x_index((i + step) % 4)) for i in range(4)])


def pairs_x(a, other):
    return lax.ppermute(a, (XL, XH), [(x_index(i), x_index(other(i))) for i in range(4)])


def swap_core(a):
    return lax.ppermute(a, C, [(0, 1), (1, 0)])


def slice_of(pos, dxh, dy):
    return ((pos[0] // 2 + dxh) % 2) * 4 + (pos[1] + dy) % 4


def cost(flops, bytes_accessed):
    return pl.CostEstimate(flops=flops, bytes_accessed=bytes_accessed, transcendentals=0)


ANY = pl.BlockSpec(memory_space=pl.ANY)
SCALARS = pl.BlockSpec(memory_space=pltpu.SMEM)


def pick_body(pos, src, out, sems):
    copies = [
        pltpu.make_async_copy(
            src.at[:, pl.ds(pl.multiple_of((2 * j + 1 - pos[2]) * PIECE, PIECE), PIECE)],
            out.at[:, j * PIECE : (j + 1) * PIECE],
            sems.at[j],
        )
        for j in range(8)
    ]
    for copy in copies:
        copy.start()
    for copy in copies:
        copy.wait()


def other_half(pos, tokens):
    return pl.pallas_call(
        pick_body,
        out_shape=jax.ShapeDtypeStruct((ROWS, DEPTH // 2), BF16),
        in_specs=[SCALARS, ANY],
        out_specs=ANY,
        scratch_shapes=[pltpu.SemaphoreType.DMA((8,))],
        compiler_params=PARAMS,
        cost_estimate=cost(0, 2**21),
    )(pos, tokens)


def partial_body(pos, tok, tok_other, cot, cot_other, in_scale, out_scale, grad_ref, *refs):
    stay, plus, minus, two_low, two_high, left = refs
    i = pl.program_id(0)

    @pl.when(i == 0)
    def _():
        grad_ref[:ROWS] = (cot[...].astype(F32) * out_scale[...]).astype(BF16)
        grad_ref[ROWS:] = (cot_other[...].astype(F32) * out_scale[...]).astype(BF16)

    y_at = (pos[1] + i) % 4
    for k in range(4):
        x_at = (pos[0] + k) % 4
        place = (x_at // 2) * 4 + y_at
        wide = pl.ds(pl.multiple_of(((place * 2 + pos[2]) * 2 + x_at % 2) * LANE, LANE), LANE)
        narrow = pl.ds(pl.multiple_of((place * 2 + x_at % 2) * LANE, LANE), LANE)
        scale = in_scale[:, wide]
        left[:ROWS, k * LANE : (k + 1) * LANE] = (tok[:, wide].astype(F32) * scale).astype(BF16)
        left[ROWS:, k * LANE : (k + 1) * LANE] = (tok_other[:, narrow].astype(F32) * scale).astype(BF16)
    part = lax.dot_general(
        left[...], grad_ref[...], (((0,), (0,)), ((), ())), preferred_element_type=F32
    ).astype(BF16)
    stay[0] = part[:LANE]
    plus[0] = part[LANE : 2 * LANE]
    two_low[0] = part[2 * LANE : 3 * LANE, :HALF]
    two_high[0] = part[2 * LANE : 3 * LANE, HALF:]
    minus[0] = part[3 * LANE :]


def partials(pos, tokens, tok_other, cot, cot_other, in_scale, out_scale):
    whole = lambda shape: pl.BlockSpec(shape, lambda i, pos: (0,) * len(shape))
    columns = (WIDTH, WIDTH, WIDTH, HALF, HALF)
    return pl.pallas_call(
        partial_body,
        out_shape=[jax.ShapeDtypeStruct((2 * ROWS, WIDTH), BF16)]
        + [jax.ShapeDtypeStruct((4, LANE, n), BF16) for n in columns],
        grid_spec=pltpu.PrefetchScalarGridSpec(
            num_scalar_prefetch=1,
            grid=(4,),
            in_specs=[
                whole((ROWS, DEPTH)), whole((ROWS, DEPTH // 2)), whole((ROWS, WIDTH)),
                whole((ROWS, WIDTH)), whole((1, DEPTH)), whole((1, WIDTH)),
            ],
            out_specs=[whole((2 * ROWS, WIDTH))]
            + [pl.BlockSpec((1, LANE, n), lambda i, pos: (i, 0, 0)) for n in columns],
            scratch_shapes=[pltpu.VMEM((2 * ROWS, 4 * LANE), BF16)],
        ),
        compiler_params=PARAMS,
        cost_estimate=cost(2 * 2 * ROWS * DEPTH // 2 * WIDTH, 9 * 2**20),
    )(pos, tokens, tok_other, cot, cot_other, in_scale, out_scale)


def add_body(plus, minus, low, high, plus_out, minus_out):
    plus_out[...] = (plus[...].astype(F32) + low[...].astype(F32)).astype(BF16)
    minus_out[...] = (minus[...].astype(F32) + high[...].astype(F32)).astype(BF16)


def add_halves(plus, minus, low, high):
    block = (4, LANE, HALF)
    first, second = pl.BlockSpec(block, lambda i: (0, 0, 0)), pl.BlockSpec(block, lambda i: (0, 0, 1))
    return pl.pallas_call(
        add_body,
        out_shape=[jax.ShapeDtypeStruct((4, LANE, WIDTH), BF16)] * 2,
        grid=(1,),
        in_specs=[first, second, first, first],
        out_specs=[first, second],
        input_output_aliases={0: 0, 1: 1},
        compiler_params=PARAMS,
        cost_estimate=cost(2**20, 3 * 2**20),
    )(plus, minus, low, high)


def sum_body(own, r1, r2, keep, s1, s2, s3):
    for k, out in enumerate((keep, s1, s2, s3)):
        out[...] = (own[k].astype(F32) + r1[k].astype(F32) + r2[k].astype(F32)).astype(out.dtype)


def sum_blocks(own, arrived):
    shape = own.shape[1:]
    return pl.pallas_call(
        sum_body,
        out_shape=[jax.ShapeDtypeStruct(shape, F32)] + [jax.ShapeDtypeStruct(shape, BF16)] * 3,
        in_specs=[VMEM] * 3,
        out_specs=[VMEM] * 4,
        compiler_params=PARAMS,
        cost_estimate=cost(2**20, 4 * 2**20),
    )(own, *arrived)


def join_body(pos, own, r1, r2, r3, keep, send):
    count = LANE // 2
    mine = pos[3] % 2
    for out, at in ((keep, mine), (send, 1 - mine)):
        rows = pl.ds(pl.multiple_of(at * count, count), count)
        total = own[rows]
        for ref in (r1, r2, r3):
            total = total + ref[rows].astype(F32)
        out[...] = total.astype(out.dtype)


def join(pos, own, arrived):
    shape = (LANE // 2, WIDTH)
    return pl.pallas_call(
        join_body,
        out_shape=[jax.ShapeDtypeStruct(shape, F32), jax.ShapeDtypeStruct(shape, BF16)],
        in_specs=[SCALARS] + [VMEM] * 4,
        out_specs=[VMEM] * 2,
        compiler_params=PARAMS,
        cost_estimate=cost(2**20, 2**21),
    )(pos, own, *arrived)


def place_body(scale, pos, own, by_z, by_x, by_both, out):
    count = LANE // 2
    me = (pos[0] % 2) * 2 + pos[3] % 2
    for flip, ref in enumerate((own, by_z, by_x, by_both)):
        at = (me // 2 + flip // 2) % 2 * 2 + (me + flip) % 2
        out[pl.ds(pl.multiple_of(at * count, count), count)] = ref[...].astype(F32) * scale


def place(pos, blocks, scale):
    return pl.pallas_call(
        functools.partial(place_body, scale),
        out_shape=jax.ShapeDtypeStruct((PIECE, WIDTH), F32),
        in_specs=[SCALARS] + [VMEM] * 4,
        out_specs=VMEM,
        compiler_params=PARAMS,
        cost_estimate=cost(2**18, 2**20),
    )(pos, *blocks)


def layer_body(order, last, pos, tok, tok_other, grad, in_scale, cot, cot_other, *refs):
    weights, refs = refs[:4], refs[4:]
    if last:
        (pre_in, small_in, _), refs = refs[:3], refs[3:]
        own_ref, other_ref, pre_ref, pre_other, small, total = refs
    else:
        own_ref, other_ref, pre_ref, small = refs
        total = pre_ref
    i = pl.program_id(0)

    @pl.when(i == 0)
    def _():
        if last:
            total[...] = pre_in[...]
            small[...] = small_in[...]
        else:
            small[...] = jnp.zeros_like(small)

    for m, (dxh, dy) in enumerate(order):
        @pl.when(i == m)
        def _():
            at = slice_of(pos, dxh, dy)
            wide = pl.ds(pl.multiple_of((at * 2 + pos[2]) * PIECE, PIECE), PIECE)
            narrow = pl.ds(pl.multiple_of(at * PIECE, PIECE), PIECE)
            scale = in_scale[:, wide]
            weight = weights[m][...]
            sums = jnp.zeros((1, PIECE), F32)
            for part, values in ((0, tok[:, wide]), (1, tok_other[:, narrow])):
                rows = slice(part * ROWS, (part + 1) * ROWS)
                values = values.astype(F32)
                scaled = (values * scale).astype(BF16)
                pre = jnp.dot(scaled, weight, preferred_element_type=F32)
                if m == 0 and not last:
                    total[rows] = pre
                else:
                    total[rows] += pre
                back = lax.dot_general(
                    grad[rows], weight, (((1,), (1,)), ((), ())), preferred_element_type=F32
                )
                (own_ref, other_ref)[part][...] = (back * scale).astype(BF16)
                sums = sums + jnp.sum(values * back, axis=0, keepdims=True)
            small[:, wide] = sums

    if last:
        @pl.when(i == 3)
        def _():
            pre_ref[...] = total[:ROWS]
            pre_other[...] = total[ROWS:].astype(BF16)
            small[:, DEPTH:] = jnp.sum(
                cot[...].astype(F32) * total[:ROWS] + cot_other[...].astype(F32) * total[ROWS:],
                axis=0, keepdims=True,
            )


def layer(pos, order, tokens, tok_other, grad, in_scale, cot, cot_other, weights, before=None):
    whole = lambda shape: pl.BlockSpec(shape, lambda i, pos: (0,) * len(shape))
    shaped = jax.ShapeDtypeStruct
    dxhs = [o[0] for o in order]
    dys = [o[1] for o in order]

    def column(i, pos):
        dxh, dy = dxhs[3], dys[3]
        for m in range(3):
            dxh = jnp.where(i == m, dxhs[m], dxh)
            dy = jnp.where(i == m, dys[m], dy)
        return 0, slice_of(pos, dxh, dy) * 2 + pos[2]

    in_specs = [
        whole((ROWS, DEPTH)), whole((ROWS, DEPTH // 2)), whole((2 * ROWS, WIDTH)), whole((1, DEPTH)),
        whole((ROWS, WIDTH)), whole((ROWS, WIDTH)),
    ] + [whole((PIECE, WIDTH))] * 4
    operands = [tokens, tok_other, grad, in_scale, cot, cot_other, *weights]
    out_shape = [shaped((ROWS, DEPTH), BF16), shaped((ROWS, DEPTH // 4), BF16)]
    out_specs = [pl.BlockSpec((ROWS, PIECE), column), pl.BlockSpec((ROWS, PIECE), lambda i, pos: (0, i))]
    scratch, aliases = [], {}
    small = shaped((1, DEPTH + WIDTH), F32)
    if before is None:
        out_shape += [shaped((2 * ROWS, WIDTH), F32), small]
        out_specs += [whole((2 * ROWS, WIDTH)), whole(small.shape)]
    else:
        own, pre, sums = before
        operands += [pre, sums, own]
        in_specs += [whole((2 * ROWS, WIDTH)), whole(small.shape), pl.BlockSpec(memory_space=pl.ANY)]
        aliases = {len(operands): 0}
        out_shape += [shaped((ROWS, WIDTH), F32), shaped((ROWS, WIDTH), BF16), small]
        out_specs += [whole((ROWS, WIDTH)), whole((ROWS, WIDTH)), whole(small.shape)]
        scratch = [pltpu.VMEM((2 * ROWS, WIDTH), F32)]
    return pl.pallas_call(
        functools.partial(layer_body, order, before is not None),
        out_shape=out_shape,
        grid_spec=pltpu.PrefetchScalarGridSpec(
            num_scalar_prefetch=1, grid=(4,), in_specs=in_specs, out_specs=out_specs,
            scratch_shapes=scratch,
        ),
        input_output_aliases=aliases,
        compiler_params=PARAMS,
        cost_estimate=cost(2 * 2 * 2 * ROWS * WIDTH * WIDTH, 10 * 2**20),
    )(pos, *operands)


def fill_body(orders, pos, first, second, _, out, sems):
    copies = []
    for b, (order, src) in enumerate(zip(orders, (first, second))):
        for m, (dxh, dy) in enumerate(order):
            at = (slice_of(pos, dxh, dy) * 2 + 1 - pos[2]) * PIECE
            copies.append(pltpu.make_async_copy(
                src.at[:, m * PIECE : (m + 1) * PIECE],
                out.at[:, pl.ds(pl.multiple_of(at, PIECE), PIECE)],
                sems.at[b * 4 + m],
            ))
    for copy in copies:
        copy.start()
    for copy in copies:
        copy.wait()


def fill(pos, orders, first, second, own):
    return pl.pallas_call(
        functools.partial(fill_body, orders),
        out_shape=jax.ShapeDtypeStruct((ROWS, DEPTH), BF16),
        in_specs=[SCALARS] + [ANY] * 3,
        out_specs=ANY,
        scratch_shapes=[pltpu.SemaphoreType.DMA((8,))],
        input_output_aliases={3: 0},
        compiler_params=PARAMS,
        cost_estimate=cost(0, 2**21),
    )(pos, first, second, own)


def finish_body(scale, mine, other, in_ref, out_ref):
    total = (mine[...] + other[...]) * scale
    in_ref[...] = total[:, :DEPTH]
    out_ref[...] = total[:, DEPTH:]


def finish(mine, other, scale):
    return pl.pallas_call(
        functools.partial(finish_body, scale),
        out_shape=[jax.ShapeDtypeStruct((1, DEPTH), F32), jax.ShapeDtypeStruct((1, WIDTH), F32)],
        in_specs=[VMEM] * 2,
        out_specs=[VMEM] * 2,
        compiler_params=PARAMS,
        cost_estimate=cost(2**14, 2**16),
    )(mine, other)


def on_device(tokens, cotangent, slow_weight, in_scale, out_scale):
    xl, z, xh, y, c = (lax.axis_index(a) for a in (XL, Z, XH, Y, C))
    pos = jnp.stack([2 * xh + xl, y, c, z]).astype(jnp.int32)
    member_norm = 1.0 / float(ROWS * 16) ** 0.5
    total_norm = 1.0 / float(ROWS * 256) ** 0.5

    cot_other = swap_core(cotangent)
    up, down = send_y(slow_weight, 1), send_y(slow_weight, -1)
    far = pairs_x(slow_weight, lambda i: 3 - i)
    tok_other = swap_core(other_half(pos, tokens))

    grad, stay, plus, minus, two_low, two_high = partials(
        pos, tokens, tok_other, cotangent, cot_other, in_scale, out_scale
    )
    low, high = send_x(two_low, 1), send_x(two_high, -1)
    far, up, down, grad = lax.optimization_barrier((far, up, down, grad))

    half = PIECE // 2
    far_up = send_y(jnp.concatenate([far, up[:half]], axis=0), 1)
    far_down = send_y(jnp.concatenate([far, down[half:]], axis=0), -1)
    orders = ((0, 0), (0, 1), (0, 3), (1, 0)), ((0, 2), (1, 3), (1, 1), (1, 2))
    own, others_1, pre, small = layer(
        pos, orders[0], tokens, tok_other, grad, in_scale, cotangent, cot_other,
        (slow_weight, down, up, far),
    )
    plus, minus = add_halves(plus, minus, low, high)
    arrived = [send_x(plus, 1), send_x(minus, -1)]
    far_up, far_down, own, others_1, pre, small, _ = lax.optimization_barrier(
        (far_up, far_down, own, others_1, pre, small, plus)
    )

    far_two_up = send_y(far_up[:half], 1)
    far_two_down = send_y(far_down[half:PIECE], -1)
    two = jnp.concatenate([far_up[PIECE:], far_down[PIECE:]], axis=0)
    far_two = jnp.concatenate([far_two_up, far_two_down], axis=0)
    own, others_2, pre_own, pre_other, small = layer(
        pos, orders[1], tokens, tok_other, grad, in_scale, cotangent, cot_other,
        (two, far_up[:PIECE], far_down[:PIECE], far_two), (own, pre, small),
    )
    arrived, own, others_2, pre_own, pre_other, small = lax.optimization_barrier(
        (arrived, own, others_2, pre_own, pre_other, small)
    )

    stay, *out = sum_blocks(stay, arrived)
    arrived = [send_y(out[0], 1), send_y(out[2], -1), send_y(out[1], 2)]
    small_in = swap_core(small)
    pre_other = swap_core(pre_other)
    others_1, others_2 = swap_core(others_1), swap_core(others_2)
    arrived, small_in = lax.optimization_barrier((arrived, small_in))

    keep, out = join(pos, stay, arrived)
    pair = lambda a: lax.ppermute(a, Z, [(i, i ^ 1) for i in range(8)])
    out = pair(out)
    small = small + small_in
    small_in = send_y(small, 2)
    out, small_in = lax.optimization_barrier((out, small_in))
    mine = (keep + out.astype(F32)).astype(BF16)
    plus, minus, across = send_z(mine, 2), send_z(mine, -2), send_z(mine, 4)
    small = small + small_in
    small_in = lax.ppermute(small, Y, [(i, i ^ 1) for i in range(4)])
    plus, minus, across, small_in = lax.optimization_barrier((plus, minus, across, small_in))
    summed = (mine.astype(F32) + across.astype(F32)) + (plus.astype(F32) + minus.astype(F32))
    summed = summed.astype(BF16)
    by_z = pair(summed)
    by_x = pairs_x(summed, lambda i: i ^ 1)
    by_both = lax.ppermute(summed, (XL, Z), [(i, i ^ 9) for i in range(16)])
    small = small + small_in
    small_far = lax.ppermute(small, XH, [(0, 1), (1, 0)])

    result = ((pre_own + pre_other.astype(F32)) * out_scale).astype(BF16)
    grad_tokens = fill(pos, orders, others_1, others_2, own)
    grad_weight = place(pos, (summed, by_z, by_x, by_both), total_norm)
    grad_in_scale, grad_out_scale = finish(small, small_far, member_norm)
    return result, grad_tokens, grad_weight, grad_in_scale, grad_out_scale


def solution(mesh):
    wide = Mesh(mesh.devices.reshape(2, 8, 2, 4, 2), (XL, Z, XH, Y, C))
    row, member, shard = P((XL, Z, XH, Y, C), None), P((XL, Z), None), P((XH, Y, C), None)
    return jax.shard_map(
        on_device,
        mesh=wide,
        in_specs=(row, row, shard, member, member),
        out_specs=(row, row, shard, member, member),
        check_vma=False,
    )
```

```python
import functools

import jax
import jax.numpy as jnp
from jax import lax
from jax.experimental import pallas as pl
from jax.experimental.pallas import tpu as pltpu
from jax.sharding import Mesh, PartitionSpec as P

F32, BF16 = jnp.float32, jnp.bfloat16
XL, Z, XH, Y, C = "xl", "z", "xh", "y", "c"
ROWS, DEPTH, WIDTH, PIECE = 256, 4096, 1024, 256
LOW, LANE = 640, PIECE // 2
HIGH = WIDTH - LOW
PASSING = 4 * 2**30
VMEM = pl.BlockSpec(memory_space=pltpu.VMEM)
PARAMS = pltpu.CompilerParams(vmem_limit_bytes=40 * 2**20)


def swap_core(a):
    return lax.ppermute(a, C, [(0, 1), (1, 0)])


def swap_y(a, flip):
    return lax.ppermute(a, Y, [(i, i ^ flip) for i in range(4)])


def x_index(place):
    return (place % 2) * 2 + place // 2


def swap_x(a, flip):
    return lax.ppermute(a, (XL, XH), [(x_index(i), x_index(i ^ flip)) for i in range(4)])


def swap_z(a, partners):
    return lax.ppermute(a, Z, list(enumerate(partners)))


NEAR = (1, 0, 3, 2, 5, 4, 7, 6)
NEXT = (7, 2, 1, 4, 3, 6, 5, 0)
FAR = (3, 6, 5, 0, 7, 2, 1, 4)


def slice_of(pos, dxh, dy):
    return ((pos[0] // 2) ^ dxh) * 4 + (pos[1] ^ dy)


def cost(flops, bytes_accessed):
    return pl.CostEstimate(flops=flops, bytes_accessed=bytes_accessed, transcendentals=0)


ANY = pl.BlockSpec(memory_space=pl.ANY)
SCALARS = pl.BlockSpec(memory_space=pltpu.SMEM)


def pick_body(pos, src, out, sems):
    copies = [
        pltpu.make_async_copy(
            src.at[:, pl.ds(pl.multiple_of((2 * j + 1 - pos[2]) * PIECE, PIECE), PIECE)],
            out.at[:, j * PIECE : (j + 1) * PIECE],
            sems.at[j],
        )
        for j in range(8)
    ]
    for copy in copies:
        copy.start()
    for copy in copies:
        copy.wait()


def other_half(pos, tokens):
    return pl.pallas_call(
        pick_body,
        out_shape=jax.ShapeDtypeStruct((ROWS, DEPTH // 2), BF16),
        in_specs=[SCALARS, ANY],
        out_specs=ANY,
        scratch_shapes=[pltpu.SemaphoreType.DMA((8,))],
        compiler_params=PARAMS,
        cost_estimate=cost(0, 2**21),
    )(pos, tokens)


def partial_body(pos, tok, tok_other, cot, cot_other, in_scale, out_scale, grad_ref, *refs):
    stay, one, early_one, three, late_one, late_three, left = refs
    i = pl.program_id(0)

    @pl.when(i == 0)
    def _():
        grad_ref[:ROWS] = (cot[...].astype(F32) * out_scale[...]).astype(BF16)
        grad_ref[ROWS:] = (cot_other[...].astype(F32) * out_scale[...]).astype(BF16)

    y_at = pos[1] ^ i
    for k in range(4):
        x_at = pos[0] ^ k
        place = (x_at // 2) * 4 + y_at
        wide = pl.ds(pl.multiple_of(((place * 2 + pos[2]) * 2 + x_at % 2) * LANE, LANE), LANE)
        narrow = pl.ds(pl.multiple_of((place * 2 + x_at % 2) * LANE, LANE), LANE)
        scale = in_scale[:, wide]
        left[:ROWS, k * LANE : (k + 1) * LANE] = (tok[:, wide].astype(F32) * scale).astype(BF16)
        left[ROWS:, k * LANE : (k + 1) * LANE] = (tok_other[:, narrow].astype(F32) * scale).astype(BF16)
    part = lax.dot_general(
        left[...], grad_ref[...], (((0,), (0,)), ((), ())), preferred_element_type=F32
    ).astype(BF16)
    stay[0] = part[:LANE]
    low, high = slice(0, LOW), slice(LOW, WIDTH)
    one[0] = part[2 * LANE : 3 * LANE, low]
    early_one[0] = part[LANE : 2 * LANE, low]
    three[0, :, :HIGH] = part[2 * LANE : 3 * LANE, high]
    three[0, :, HIGH:] = part[3 * LANE :, high]
    late_one[0] = part[LANE : 2 * LANE, high]
    late_three[0] = part[3 * LANE :, low]


def partials(pos, tokens, tok_other, cot, cot_other, in_scale, out_scale):
    whole = lambda shape: pl.BlockSpec(shape, lambda i, pos: (0,) * len(shape))
    columns = (WIDTH, LOW, LOW, 2 * HIGH, HIGH, LOW)
    return pl.pallas_call(
        partial_body,
        out_shape=[jax.ShapeDtypeStruct((2 * ROWS, WIDTH), BF16)]
        + [jax.ShapeDtypeStruct((4, LANE, n), BF16) for n in columns],
        grid_spec=pltpu.PrefetchScalarGridSpec(
            num_scalar_prefetch=1,
            grid=(4,),
            in_specs=[
                whole((ROWS, DEPTH)), whole((ROWS, DEPTH // 2)), whole((ROWS, WIDTH)),
                whole((ROWS, WIDTH)), whole((1, DEPTH)), whole((1, WIDTH)),
            ],
            out_specs=[whole((2 * ROWS, WIDTH))]
            + [pl.BlockSpec((1, LANE, n), lambda i, pos: (i, 0, 0)) for n in columns],
            scratch_shapes=[pltpu.VMEM((2 * ROWS, 4 * LANE), BF16)],
        ),
        compiler_params=PARAMS,
        cost_estimate=cost(2 * 2 * ROWS * DEPTH // 2 * WIDTH, 9 * 2**20),
    )(pos, tokens, tok_other, cot, cot_other, in_scale, out_scale)


def add_body(late_one, late_three, one, three, one_out, three_out):
    one_out[...] = (late_one[...].astype(F32) + three[:, :, :HIGH].astype(F32)).astype(BF16)
    three_out[...] = (late_three[...].astype(F32) + one[...].astype(F32)).astype(BF16)


def add_passing(late_one, late_three, one, three):
    return pl.pallas_call(
        add_body,
        out_shape=[jax.ShapeDtypeStruct(late_one.shape, BF16), jax.ShapeDtypeStruct(late_three.shape, BF16)],
        in_specs=[VMEM] * 4,
        out_specs=[VMEM] * 2,
        compiler_params=PARAMS,
        cost_estimate=cost(PASSING, 3 * 2**20),
    )(late_one, late_three, one, three)


def sum_body(own, early_one, three, late_one, late_three, keep, s1, s2, s3):
    low, high = slice(0, LOW), slice(LOW, WIDTH)
    for k, out in enumerate((keep, s1, s2, s3)):
        for at, early, late in ((low, early_one[k], late_three[k]), (high, three[k, :, HIGH:], late_one[k])):
            total = own[k, :, at].astype(F32) + early.astype(F32) + late.astype(F32)
            out[:, at] = total.astype(out.dtype)


def sum_blocks(own, arrived):
    shape = own.shape[1:]
    return pl.pallas_call(
        sum_body,
        out_shape=[jax.ShapeDtypeStruct(shape, F32)] + [jax.ShapeDtypeStruct(shape, BF16)] * 3,
        in_specs=[VMEM] * 5,
        out_specs=[VMEM] * 4,
        compiler_params=PARAMS,
        cost_estimate=cost(2**20, 4 * 2**20),
    )(own, *arrived)


def join_body(pos, own, r1, r2, r3, keep, send):
    count = LANE // 2
    mine = pos[3]
    for out, at in ((keep, mine), (send, 1 - mine)):
        rows = pl.ds(pl.multiple_of(at * count, count), count)
        total = own[rows]
        for ref in (r1, r2, r3):
            total = total + ref[rows].astype(F32)
        out[...] = total.astype(out.dtype)


def join(pos, own, arrived):
    shape = (LANE // 2, WIDTH)
    return pl.pallas_call(
        join_body,
        out_shape=[jax.ShapeDtypeStruct(shape, F32), jax.ShapeDtypeStruct(shape, BF16)],
        in_specs=[SCALARS] + [VMEM] * 4,
        out_specs=[VMEM] * 2,
        compiler_params=PARAMS,
        cost_estimate=cost(2**20, 2**21),
    )(pos, own, *arrived)


def place_body(scale, pos, own, by_z, by_x, by_both, out):
    count = LANE // 2
    me = (pos[0] % 2) * 2 + pos[3]
    for flip, ref in enumerate((own, by_z, by_x, by_both)):
        at = me ^ flip
        out[pl.ds(pl.multiple_of(at * count, count), count)] = ref[...].astype(F32) * scale


def place(pos, blocks, scale):
    return pl.pallas_call(
        functools.partial(place_body, scale),
        out_shape=jax.ShapeDtypeStruct((PIECE, WIDTH), F32),
        in_specs=[SCALARS] + [VMEM] * 4,
        out_specs=VMEM,
        compiler_params=PARAMS,
        cost_estimate=cost(2**18, 2**20),
    )(pos, *blocks)


def layer_body(order, first, last, pos, tok, tok_other, grad, in_scale, cot, cot_other, *refs):
    count = len(order)
    weights, refs = refs[:count], refs[count:]
    if not first:
        (pre_in, small_in), refs = refs[:2], refs[4:]
    own_ref, other_ref, small = refs[:3]
    if last:
        pre_ref, pre_other, total = refs[3:]
    else:
        (total,) = refs[3:]
    i = pl.program_id(0)

    @pl.when(i == 0)
    def _():
        if first:
            small[...] = jnp.zeros_like(small)
        else:
            total[...] = pre_in[...]
            small[...] = small_in[...]

    for m, (dxh, dy) in enumerate(order):
        @pl.when(i == m)
        def _():
            at = slice_of(pos, dxh, dy)
            wide = pl.ds(pl.multiple_of((at * 2 + pos[2]) * PIECE, PIECE), PIECE)
            narrow = pl.ds(pl.multiple_of(at * PIECE, PIECE), PIECE)
            scale = in_scale[:, wide]
            weight = weights[m][...]
            sums = jnp.zeros((1, PIECE), F32)
            for part, values in ((0, tok[:, wide]), (1, tok_other[:, narrow])):
                rows = slice(part * ROWS, (part + 1) * ROWS)
                values = values.astype(F32)
                scaled = (values * scale).astype(BF16)
                pre = jnp.dot(scaled, weight, preferred_element_type=F32)
                if m == 0 and first:
                    total[rows] = pre
                else:
                    total[rows] += pre
                back = lax.dot_general(
                    grad[rows], weight, (((1,), (1,)), ((), ())), preferred_element_type=F32
                )
                (own_ref, other_ref)[part][...] = (back * scale).astype(BF16)
                sums = sums + jnp.sum(values * back, axis=0, keepdims=True)
            place = at * 2 + pos[2]
            lane = pl.ds(pl.multiple_of((place % 4) * PIECE, PIECE), PIECE)
            small[pl.ds(place // 4, 1), lane] = sums

    if last:
        @pl.when(i == count - 1)
        def _():
            pre_ref[...] = total[:ROWS]
            pre_other[...] = total[ROWS:].astype(BF16)
            small[4:5] = jnp.sum(
                cot[...].astype(F32) * total[:ROWS] + cot_other[...].astype(F32) * total[ROWS:],
                axis=0, keepdims=True,
            )


def layer(pos, orders, step, tokens, tok_other, grad, in_scale, cot, cot_other, weights, before=()):
    whole = lambda shape: pl.BlockSpec(shape, lambda i, pos: (0,) * len(shape))
    shaped = jax.ShapeDtypeStruct
    order, first, last = orders[step], step == 0, step == len(orders) - 1
    start = sum(map(len, orders[:step]))

    def column(i, pos):
        dxh, dy = order[-1]
        for m, flips in enumerate(order[:-1]):
            dxh = jnp.where(i == m, flips[0], dxh)
            dy = jnp.where(i == m, flips[1], dy)
        return 0, slice_of(pos, dxh, dy) * 2 + pos[2]

    both, half = (2 * ROWS, WIDTH), (ROWS, WIDTH)
    small = (8, WIDTH)
    in_specs = [
        whole((ROWS, DEPTH)), whole((ROWS, DEPTH // 2)), whole(both), whole((1, DEPTH)), whole(half), whole(half),
    ] + [whole((PIECE, WIDTH))] * len(order)
    operands = [tokens, tok_other, grad, in_scale, cot, cot_other, *weights]
    aliases = {}
    if not first:
        own, others, sums, pre = before
        aliases = {len(operands) + 3: 0, len(operands) + 4: 1}
        operands += [pre, sums, own, others]
        in_specs += [whole(both), whole(small), ANY, ANY]
    out_shape = [shaped((ROWS, DEPTH), BF16), shaped((ROWS, DEPTH // 2), BF16), shaped(small, F32)]
    out_specs = [
        pl.BlockSpec((ROWS, PIECE), column),
        pl.BlockSpec((ROWS, PIECE), lambda i, pos: (0, i + start)),
        whole(small),
    ]
    if last:
        out_shape += [shaped(half, F32), shaped(half, BF16)]
        out_specs += [whole(half), whole(half)]
    else:
        out_shape += [shaped(both, F32)]
        out_specs += [whole(both)]
    return pl.pallas_call(
        functools.partial(layer_body, order, first, last),
        out_shape=out_shape,
        grid_spec=pltpu.PrefetchScalarGridSpec(
            num_scalar_prefetch=1, grid=(len(order),), in_specs=in_specs, out_specs=out_specs,
            scratch_shapes=[pltpu.VMEM(both, F32)] if last else [],
        ),
        input_output_aliases=aliases,
        compiler_params=PARAMS,
        cost_estimate=cost(1, 1),
    )(pos, *operands)


def fill_body(flips, pos, src, _, out, sems):
    copies = []
    for m, (dxh, dy) in enumerate(flips):
        at = (slice_of(pos, dxh, dy) * 2 + 1 - pos[2]) * PIECE
        copies.append(pltpu.make_async_copy(
            src.at[:, m * PIECE : (m + 1) * PIECE],
            out.at[:, pl.ds(pl.multiple_of(at, PIECE), PIECE)],
            sems.at[m],
        ))
    for copy in copies:
        copy.start()
    for copy in copies:
        copy.wait()


def fill(pos, flips, others, own):
    return pl.pallas_call(
        functools.partial(fill_body, flips),
        out_shape=jax.ShapeDtypeStruct((ROWS, DEPTH), BF16),
        in_specs=[SCALARS, ANY, ANY],
        out_specs=ANY,
        scratch_shapes=[pltpu.SemaphoreType.DMA((8,))],
        input_output_aliases={2: 0},
        compiler_params=PARAMS,
        cost_estimate=cost(0, 2**21),
    )(pos, others, own)


def finish_body(scale, mine, other, in_ref, out_ref):
    total = (mine[...] + other[...]) * scale
    for k in range(4):
        in_ref[:, k * WIDTH : (k + 1) * WIDTH] = total[k : k + 1]
    out_ref[...] = total[4:5]


def finish(mine, other, scale):
    return pl.pallas_call(
        functools.partial(finish_body, scale),
        out_shape=[jax.ShapeDtypeStruct((1, DEPTH), F32), jax.ShapeDtypeStruct((1, WIDTH), F32)],
        in_specs=[VMEM] * 2,
        out_specs=[VMEM] * 2,
        compiler_params=PARAMS,
        cost_estimate=cost(2**14, 2**16),
    )(mine, other)


def on_device(tokens, cotangent, slow_weight, in_scale, out_scale):
    xl, z, xh, y, c = (lax.axis_index(a) for a in (XL, Z, XH, Y, C))
    pos = jnp.stack([2 * xh + xl, y, c, (z ^ (z // 2)) % 2]).astype(jnp.int32)
    member_norm = 1.0 / float(ROWS * 16) ** 0.5
    total_norm = 1.0 / float(ROWS * 256) ** 0.5

    cot_other = swap_core(cotangent)
    one, three = swap_y(slow_weight, 1), swap_y(slow_weight, 3)
    far = swap_x(slow_weight, 3)
    tok_other = swap_core(other_half(pos, tokens))
    grad, stay, by_one, early_one, by_three, late_one, late_three = partials(
        pos, tokens, tok_other, cotangent, cot_other, in_scale, out_scale
    )
    by_one, early_one, by_three = swap_x(by_one, 1), swap_x(early_one, 1), swap_x(by_three, 3)
    far, one, three, grad = lax.optimization_barrier((far, one, three, grad))

    half = PIECE // 2
    far_one = swap_y(jnp.concatenate([far, three[:half]], axis=0), 1)
    far_three = swap_y(jnp.concatenate([far, one[half:]], axis=0), 3)
    orders = ((0, 0), (0, 1), (0, 3), (1, 0)), ((0, 2), (1, 1), (1, 3)), ((1, 2),)
    run = functools.partial(layer, pos, orders)
    common = (tokens, tok_other, grad, in_scale, cotangent, cot_other)
    state = run(0, *common, (slow_weight, one, three, far))
    late_one, late_three = add_passing(late_one, late_three, by_one, by_three)
    arrived = [early_one, by_three, swap_x(late_one, 1), swap_x(late_three, 3)]
    far_one, far_three, state, _ = lax.optimization_barrier((far_one, far_three, state, late_one))

    far_two = [swap_y(far_three[:half], 1), swap_y(far_one[half:PIECE], 3)]
    two = jnp.concatenate([far_one[PIECE:], far_three[PIECE:]], axis=0)
    state = run(1, *common, (two, far_one[:PIECE], far_three[:PIECE]), state)
    far_two, state = lax.optimization_barrier((far_two, state))
    state = run(2, *common, (jnp.concatenate(far_two, axis=0),), state)
    arrived, state = lax.optimization_barrier((arrived, state))
    own, others, small, pre_own, pre_other = state

    stay, *out = sum_blocks(stay, arrived)
    arrived = [swap_y(out[0], 1), swap_y(out[2], 3), swap_y(out[1], 2)]
    small = small + swap_core(small)
    small = small + swap_y(small, 1)
    arrived, small = lax.optimization_barrier((arrived, small))

    keep, out = join(pos, stay, arrived)
    out = swap_z(out, NEAR)
    pre_other, others = swap_core(pre_other), swap_core(others)
    out, small = lax.optimization_barrier((out, small))
    mine = (keep + out.astype(F32)).astype(BF16)
    out = swap_z(mine, NEXT)
    small = small + swap_y(small, 3)
    out, small = lax.optimization_barrier((out, small))
    mine = (mine.astype(F32) + out.astype(F32)).astype(BF16)
    out = swap_z(mine, FAR)
    small_far = swap_x(small, 2)
    result = ((pre_own + pre_other.astype(F32)) * out_scale).astype(BF16)
    grad_tokens = fill(pos, sum(orders, ()), others, own)
    out, small_far, result, grad_tokens = lax.optimization_barrier((out, small_far, result, grad_tokens))
    mine = (mine.astype(F32) + out.astype(F32)).astype(BF16)
    by_z, by_x = swap_z(mine, NEAR), swap_x(mine, 1)
    by_both = lax.ppermute(mine, (XL, Z), [(i, i ^ 9) for i in range(16)])
    grad_in_scale, grad_out_scale = finish(small, small_far, member_norm)
    grad_weight = place(pos, (mine, by_z, by_x, by_both), total_norm)
    return result, grad_tokens, grad_weight, grad_in_scale, grad_out_scale


def solution(mesh):
    wide = Mesh(mesh.devices.reshape(2, 8, 2, 4, 2), (XL, Z, XH, Y, C))
    row, member, shard = P((XL, Z, XH, Y, C), None), P((XL, Z), None), P((XH, Y, C), None)
    return jax.shard_map(
        on_device,
        mesh=wide,
        in_specs=(row, row, shard, member, member),
        out_specs=(row, row, shard, member, member),
        check_vma=False,
    )
```

```python
import functools

import jax
import jax.numpy as jnp
from jax import lax
from jax.experimental import pallas as pl
from jax.experimental.pallas import tpu as pltpu
from jax.sharding import Mesh, PartitionSpec as P

F32, BF16 = jnp.float32, jnp.bfloat16
XL, Z, XH, Y, C = "xl", "z", "xh", "y", "c"
ROWS, DEPTH, WIDTH, PIECE = 256, 4096, 1024, 256
LOW, LANE = 640, PIECE // 2
HIGH = WIDTH - LOW
PASSING = 2 * 2**30
VMEM = pl.BlockSpec(memory_space=pltpu.VMEM)
PARAMS = pltpu.CompilerParams(vmem_limit_bytes=40 * 2**20)


def swap_core(a):
    return lax.ppermute(a, C, [(0, 1), (1, 0)])


BOTH, ONE = (0, 1), (1,)


def swap_y(a, flip, cores=BOTH):
    return lax.ppermute(a, (Y, C), [(i * 2 + c, (i ^ flip) * 2 + c) for i in range(4) for c in cores])


def x_index(place):
    return (place % 2) * 2 + place // 2


def swap_x(a, flip, cores=BOTH):
    pairs = [(x_index(i), x_index(i ^ flip)) for i in range(4)]
    return lax.ppermute(a, (XL, XH, C), [(i * 2 + c, j * 2 + c) for i, j in pairs for c in cores])


def swap_z(a, partners):
    return lax.ppermute(a, Z, list(enumerate(partners)))


NEAR = (1, 0, 3, 2, 5, 4, 7, 6)
NEXT = (7, 2, 1, 4, 3, 6, 5, 0)
FAR = (3, 6, 5, 0, 7, 2, 1, 4)


def slice_of(pos, dxh, dy):
    return ((pos[0] // 2) ^ dxh) * 4 + (pos[1] ^ dy)


def cost(flops, bytes_accessed):
    return pl.CostEstimate(flops=flops, bytes_accessed=bytes_accessed, transcendentals=0)


ANY = pl.BlockSpec(memory_space=pl.ANY)
SCALARS = pl.BlockSpec(memory_space=pltpu.SMEM)


def pick_body(pos, src, out, sems):
    copies = [
        pltpu.make_async_copy(
            src.at[:, pl.ds(pl.multiple_of((2 * j + 1 - pos[2]) * PIECE, PIECE), PIECE)],
            out.at[:, j * PIECE : (j + 1) * PIECE],
            sems.at[j],
        )
        for j in range(8)
    ]
    for copy in copies:
        copy.start()
    for copy in copies:
        copy.wait()


def other_half(pos, tokens):
    return pl.pallas_call(
        pick_body,
        out_shape=jax.ShapeDtypeStruct((ROWS, DEPTH // 2), BF16),
        in_specs=[SCALARS, ANY],
        out_specs=ANY,
        scratch_shapes=[pltpu.SemaphoreType.DMA((8,))],
        compiler_params=PARAMS,
        cost_estimate=cost(0, 2**21),
    )(pos, tokens)


def scaled_pieces(pos, flips, tok, tok_other, in_scale, left):
    y_at = pos[1] ^ pl.program_id(0)
    for n, k in enumerate(flips):
        x_at = pos[0] ^ k
        place = (x_at // 2) * 4 + y_at
        wide = pl.ds(pl.multiple_of(((place * 2 + pos[2]) * 2 + x_at % 2) * LANE, LANE), LANE)
        narrow = pl.ds(pl.multiple_of((place * 2 + x_at % 2) * LANE, LANE), LANE)
        scale = in_scale[:, wide]
        left[:ROWS, n * LANE : (n + 1) * LANE] = (tok[:, wide].astype(F32) * scale).astype(BF16)
        left[ROWS:, n * LANE : (n + 1) * LANE] = (tok_other[:, narrow].astype(F32) * scale).astype(BF16)


def product(left, grad):
    return lax.dot_general(left, grad, (((0,), (0,)), ((), ())), preferred_element_type=F32).astype(BF16)


def first_body(pos, tok, tok_other, in_scale, cot, cot_other, out_scale, grad_ref, one, three, left):
    @pl.when(pl.program_id(0) == 0)
    def _():
        grad_ref[:ROWS] = (cot[...].astype(F32) * out_scale[...]).astype(BF16)
        grad_ref[ROWS:] = (cot_other[...].astype(F32) * out_scale[...]).astype(BF16)

    scaled_pieces(pos, (2, 3), tok, tok_other, in_scale, left)
    one[0] = product(left[:, :LANE], grad_ref[:, :LOW])
    part = product(left[...], grad_ref[:, LOW:])
    three[0, :, :HIGH] = part[:LANE]
    three[0, :, HIGH:] = part[LANE:]


def rest_body(pos, tok, tok_other, in_scale, grad_ref, stay, early_one, late_one, late_three, left):
    scaled_pieces(pos, (0, 1, 3), tok, tok_other, in_scale, left)
    part = product(left[:, : 2 * LANE], grad_ref[...])
    stay[0] = part[:LANE]
    early_one[0] = part[LANE:, :LOW]
    late_one[0] = part[LANE:, LOW:]
    late_three[0] = product(left[:, 2 * LANE :], grad_ref[:, :LOW])


def partials(body, pieces, columns, pos, tokens, tok_other, in_scale, grads):
    whole = lambda shape: pl.BlockSpec(shape, lambda i, pos: (0,) * len(shape))
    out_shape = [jax.ShapeDtypeStruct((4, LANE, n), BF16) for n in columns]
    out_specs = [pl.BlockSpec((1, LANE, n), lambda i, pos: (i, 0, 0)) for n in columns]
    if len(grads) > 1:
        out_shape = [jax.ShapeDtypeStruct((2 * ROWS, WIDTH), BF16)] + out_shape
        out_specs = [whole((2 * ROWS, WIDTH))] + out_specs
    return pl.pallas_call(
        body,
        out_shape=out_shape,
        grid_spec=pltpu.PrefetchScalarGridSpec(
            num_scalar_prefetch=1,
            grid=(4,),
            in_specs=[whole((ROWS, DEPTH)), whole((ROWS, DEPTH // 2)), whole((1, DEPTH))]
            + [whole(g.shape) for g in grads],
            out_specs=out_specs,
            scratch_shapes=[pltpu.VMEM((2 * ROWS, pieces * LANE), BF16)],
        ),
        compiler_params=PARAMS,
        cost_estimate=cost(2 * ROWS * DEPTH // 2 * WIDTH, 5 * 2**20),
    )(pos, tokens, tok_other, in_scale, *grads)


def add_body(late, passing, out):
    out[...] = (late[...].astype(F32) + passing[:, :, : out.shape[2]].astype(F32)).astype(BF16)


def add_passing(late, passing):
    return pl.pallas_call(
        add_body,
        out_shape=jax.ShapeDtypeStruct(late.shape, BF16),
        in_specs=[VMEM] * 2,
        out_specs=VMEM,
        compiler_params=PARAMS,
        cost_estimate=cost(PASSING, 3 * 2**20),
    )(late, passing)


def sum_body(own, early_one, three, late_one, late_three, keep, s1, s2, s3):
    low, high = slice(0, LOW), slice(LOW, WIDTH)
    for k, out in enumerate((keep, s1, s2, s3)):
        for at, early, late in ((low, early_one[k], late_three[k]), (high, three[k, :, HIGH:], late_one[k])):
            total = own[k, :, at].astype(F32) + early.astype(F32) + late.astype(F32)
            out[:, at] = total.astype(out.dtype)


def sum_blocks(own, arrived):
    shape = own.shape[1:]
    return pl.pallas_call(
        sum_body,
        out_shape=[jax.ShapeDtypeStruct(shape, F32)] + [jax.ShapeDtypeStruct(shape, BF16)] * 3,
        in_specs=[VMEM] * 5,
        out_specs=[VMEM] * 4,
        compiler_params=PARAMS,
        cost_estimate=cost(2**20, 4 * 2**20),
    )(own, *arrived)


def join_body(pos, own, r1, r2, r3, keep, send):
    count = LANE // 2
    mine = pos[3]
    for out, at in ((keep, mine), (send, 1 - mine)):
        rows = pl.ds(pl.multiple_of(at * count, count), count)
        total = own[rows]
        for ref in (r1, r2, r3):
            total = total + ref[rows].astype(F32)
        out[...] = total.astype(out.dtype)


def join(pos, own, arrived):
    shape = (LANE // 2, WIDTH)
    return pl.pallas_call(
        join_body,
        out_shape=[jax.ShapeDtypeStruct(shape, F32), jax.ShapeDtypeStruct(shape, BF16)],
        in_specs=[SCALARS] + [VMEM] * 4,
        out_specs=[VMEM] * 2,
        compiler_params=PARAMS,
        cost_estimate=cost(2**20, 2**21),
    )(pos, own, *arrived)


def place_body(scale, pos, own, by_z, by_x, by_both, out):
    count = LANE // 2
    me = (pos[0] % 2) * 2 + pos[3]
    for flip, ref in enumerate((own, by_z, by_x, by_both)):
        at = me ^ flip
        out[pl.ds(pl.multiple_of(at * count, count), count)] = ref[...].astype(F32) * scale


def place(pos, blocks, scale):
    return pl.pallas_call(
        functools.partial(place_body, scale),
        out_shape=jax.ShapeDtypeStruct((PIECE, WIDTH), F32),
        in_specs=[SCALARS] + [VMEM] * 4,
        out_specs=VMEM,
        compiler_params=PARAMS,
        cost_estimate=cost(2**18, 2**20),
    )(pos, *blocks)


def layer_body(order, first, last, pos, tok, tok_other, grad, in_scale, cot, cot_other, *refs):
    count = len(order)
    weights, refs = refs[:count], refs[count:]
    if not first:
        (pre_in, small_in), refs = refs[:2], refs[4:]
    own_ref, other_ref, small = refs[:3]
    if last:
        pre_ref, pre_other, total = refs[3:]
    else:
        (total,) = refs[3:]
    i = pl.program_id(0)

    @pl.when(i == 0)
    def _():
        if first:
            small[...] = jnp.zeros_like(small)
        else:
            total[...] = pre_in[...]
            small[...] = small_in[...]

    for m, (dxh, dy) in enumerate(order):
        @pl.when(i == m)
        def _():
            at = slice_of(pos, dxh, dy)
            wide = pl.ds(pl.multiple_of((at * 2 + pos[2]) * PIECE, PIECE), PIECE)
            narrow = pl.ds(pl.multiple_of(at * PIECE, PIECE), PIECE)
            scale = in_scale[:, wide]
            weight = weights[m][...]
            sums = jnp.zeros((1, PIECE), F32)
            for part, values in ((0, tok[:, wide]), (1, tok_other[:, narrow])):
                rows = slice(part * ROWS, (part + 1) * ROWS)
                values = values.astype(F32)
                scaled = (values * scale).astype(BF16)
                pre = jnp.dot(scaled, weight, preferred_element_type=F32)
                if m == 0 and first:
                    total[rows] = pre
                else:
                    total[rows] += pre
                back = lax.dot_general(
                    grad[rows], weight, (((1,), (1,)), ((), ())), preferred_element_type=F32
                )
                (own_ref, other_ref)[part][...] = (back * scale).astype(BF16)
                sums = sums + jnp.sum(values * back, axis=0, keepdims=True)
            place = at * 2 + pos[2]
            lane = pl.ds(pl.multiple_of((place % 4) * PIECE, PIECE), PIECE)
            small[pl.ds(place // 4, 1), lane] = sums

    if last:
        @pl.when(i == count - 1)
        def _():
            pre_ref[...] = total[:ROWS]
            pre_other[...] = total[ROWS:].astype(BF16)
            small[4:5] = jnp.sum(
                cot[...].astype(F32) * total[:ROWS] + cot_other[...].astype(F32) * total[ROWS:],
                axis=0, keepdims=True,
            )


def layer(pos, orders, step, tokens, tok_other, grad, in_scale, cot, cot_other, weights, before=()):
    whole = lambda shape: pl.BlockSpec(shape, lambda i, pos: (0,) * len(shape))
    shaped = jax.ShapeDtypeStruct
    order, first, last = orders[step], step == 0, step == len(orders) - 1
    start = sum(map(len, orders[:step]))

    def column(i, pos):
        dxh, dy = order[-1]
        for m, flips in enumerate(order[:-1]):
            dxh = jnp.where(i == m, flips[0], dxh)
            dy = jnp.where(i == m, flips[1], dy)
        return 0, slice_of(pos, dxh, dy) * 2 + pos[2]

    both, half = (2 * ROWS, WIDTH), (ROWS, WIDTH)
    small = (8, WIDTH)
    in_specs = [
        whole((ROWS, DEPTH)), whole((ROWS, DEPTH // 2)), whole(both), whole((1, DEPTH)), whole(half), whole(half),
    ] + [whole((PIECE, WIDTH))] * len(order)
    operands = [tokens, tok_other, grad, in_scale, cot, cot_other, *weights]
    aliases = {}
    if not first:
        own, others, sums, pre = before
        aliases = {len(operands) + 3: 0, len(operands) + 4: 1}
        operands += [pre, sums, own, others]
        in_specs += [whole(both), whole(small), ANY, ANY]
    out_shape = [shaped((ROWS, DEPTH), BF16), shaped((ROWS, DEPTH // 2), BF16), shaped(small, F32)]
    out_specs = [
        pl.BlockSpec((ROWS, PIECE), column),
        pl.BlockSpec((ROWS, PIECE), lambda i, pos: (0, i + start)),
        whole(small),
    ]
    if last:
        out_shape += [shaped(half, F32), shaped(half, BF16)]
        out_specs += [whole(half), whole(half)]
    else:
        out_shape += [shaped(both, F32)]
        out_specs += [whole(both)]
    return pl.pallas_call(
        functools.partial(layer_body, order, first, last),
        out_shape=out_shape,
        grid_spec=pltpu.PrefetchScalarGridSpec(
            num_scalar_prefetch=1, grid=(len(order),), in_specs=in_specs, out_specs=out_specs,
            scratch_shapes=[pltpu.VMEM(both, F32)] if last else [],
        ),
        input_output_aliases=aliases,
        compiler_params=PARAMS,
        cost_estimate=cost(1, 1),
    )(pos, *operands)


def fill_body(flips, pos, src, _, out, sems):
    copies = []
    for m, (dxh, dy) in enumerate(flips):
        at = (slice_of(pos, dxh, dy) * 2 + 1 - pos[2]) * PIECE
        copies.append(pltpu.make_async_copy(
            src.at[:, m * PIECE : (m + 1) * PIECE],
            out.at[:, pl.ds(pl.multiple_of(at, PIECE), PIECE)],
            sems.at[m],
        ))
    for copy in copies:
        copy.start()
    for copy in copies:
        copy.wait()


def fill(pos, flips, others, own):
    return pl.pallas_call(
        functools.partial(fill_body, flips),
        out_shape=jax.ShapeDtypeStruct((ROWS, DEPTH), BF16),
        in_specs=[SCALARS, ANY, ANY],
        out_specs=ANY,
        scratch_shapes=[pltpu.SemaphoreType.DMA((8,))],
        input_output_aliases={2: 0},
        compiler_params=PARAMS,
        cost_estimate=cost(0, 2**21),
    )(pos, others, own)


def finish_body(scale, pos, mine, other, in_ref, out_ref):
    total = jnp.where(pos[2] == 1, mine[...], other[...]) * scale
    for k in range(4):
        in_ref[:, k * WIDTH : (k + 1) * WIDTH] = total[k : k + 1]
    out_ref[...] = total[4:5]


def finish(pos, mine, other, scale):
    return pl.pallas_call(
        functools.partial(finish_body, scale),
        out_shape=[jax.ShapeDtypeStruct((1, DEPTH), F32), jax.ShapeDtypeStruct((1, WIDTH), F32)],
        in_specs=[SCALARS] + [VMEM] * 2,
        out_specs=[VMEM] * 2,
        compiler_params=PARAMS,
        cost_estimate=cost(2**14, 2**16),
    )(pos, mine, other)


def on_device(tokens, cotangent, slow_weight, in_scale, out_scale):
    xl, z, xh, y, c = (lax.axis_index(a) for a in (XL, Z, XH, Y, C))
    pos = jnp.stack([2 * xh + xl, y, c, (z ^ (z // 2)) % 2]).astype(jnp.int32)
    member_norm = 1.0 / float(ROWS * 16) ** 0.5
    total_norm = 1.0 / float(ROWS * 256) ** 0.5

    cot_other = swap_core(cotangent)
    one, three = swap_y(slow_weight, 1), swap_y(slow_weight, 3)
    far = swap_x(slow_weight, 3)
    tok_other = swap_core(other_half(pos, tokens))
    grad, by_one, by_three = partials(
        first_body, 2, (LOW, 2 * HIGH), pos, tokens, tok_other, in_scale, (cotangent, cot_other, out_scale)
    )
    by_one, by_three = swap_x(by_one, 1), swap_x(by_three, 3)
    stay, early_one, late_one, late_three = partials(
        rest_body, 3, (WIDTH, LOW, HIGH, LOW), pos, tokens, tok_other, in_scale, (grad,)
    )
    early_one = swap_x(early_one, 1)
    far, one, three, grad, stay = lax.optimization_barrier((far, one, three, grad, stay))

    half = PIECE // 2
    far_one = swap_y(jnp.concatenate([far, three[:half]], axis=0), 1)
    far_three = swap_y(jnp.concatenate([far, one[half:]], axis=0), 3)
    orders = ((0, 0), (0, 1), (0, 3), (1, 0)), ((0, 2), (1, 1), (1, 3)), ((1, 2),)
    run = functools.partial(layer, pos, orders)
    common = (tokens, tok_other, grad, in_scale, cotangent, cot_other)
    state = run(0, *common, (slow_weight, one, three, far))
    late_three = add_passing(late_three, by_one)
    late_one = add_passing(late_one, by_three)
    arrived = [early_one, by_three, swap_x(late_one, 1), swap_x(late_three, 3)]
    far_one, far_three, state, _ = lax.optimization_barrier((far_one, far_three, state, late_one))

    far_two = [swap_y(far_three[:half], 1), swap_y(far_one[half:PIECE], 3)]
    two = jnp.concatenate([far_one[PIECE:], far_three[PIECE:]], axis=0)
    state = run(1, *common, (two, far_one[:PIECE], far_three[:PIECE]), state)
    far_two, state = lax.optimization_barrier((far_two, state))
    arrived, _ = lax.optimization_barrier((arrived, state[3]))
    state = run(2, *common, (jnp.concatenate(far_two, axis=0),), state)
    own, others, small, pre_own, pre_other = state

    stay, *out = sum_blocks(stay, arrived)
    two = swap_y(out[1], 2)
    arrived = [two, swap_y(out[0], 1), swap_y(out[2], 3)]
    small = small + swap_core(small)
    small = small + swap_y(small, 1, ONE)
    arrived, small = lax.optimization_barrier((arrived, small))

    keep, out = join(pos, stay, arrived)
    out = swap_z(out, NEAR)
    small = small + swap_y(small, 3, ONE)
    out, small = lax.optimization_barrier((out, small))
    mine = (keep + out.astype(F32)).astype(BF16)
    out = swap_z(mine, NEXT)
    small = small + swap_x(small, 2, ONE)
    out, small = lax.optimization_barrier((out, small))
    pre_other, others = swap_core(pre_other), swap_core(others)
    mine = (mine.astype(F32) + out.astype(F32)).astype(BF16)
    out = swap_z(mine, FAR)
    result = ((pre_own + pre_other.astype(F32)) * out_scale).astype(BF16)
    grad_tokens = fill(pos, sum(orders, ()), others, own)
    out, small, result, grad_tokens = lax.optimization_barrier((out, small, result, grad_tokens))
    mine = (mine.astype(F32) + out.astype(F32)).astype(BF16)
    by_z, by_x = swap_z(mine, NEAR), swap_x(mine, 1)
    by_both = lax.ppermute(mine, (XL, Z), [(i, i ^ 9) for i in range(16)])
    small_one = lax.ppermute(small, C, [(1, 0)])
    grad_in_scale, grad_out_scale = finish(pos, small, small_one, member_norm)
    grad_weight = place(pos, (mine, by_z, by_x, by_both), total_norm)
    return result, grad_tokens, grad_weight, grad_in_scale, grad_out_scale


def solution(mesh):
    wide = Mesh(mesh.devices.reshape(2, 8, 2, 4, 2), (XL, Z, XH, Y, C))
    row, member, shard = P((XL, Z, XH, Y, C), None), P((XL, Z), None), P((XH, Y, C), None)
    return jax.shard_map(
        on_device,
        mesh=wide,
        in_specs=(row, row, shard, member, member),
        out_specs=(row, row, shard, member, member),
        check_vma=False,
    )
```

```python
import functools

import jax
import jax.numpy as jnp
from jax import lax
from jax.experimental import pallas as pl
from jax.experimental.pallas import tpu as pltpu
from jax.sharding import Mesh, PartitionSpec as P

F32, BF16 = jnp.float32, jnp.bfloat16
XL, Z, XH, Y, C = "xl", "z", "xh", "y", "c"
ROWS, DEPTH, WIDTH, PIECE = 256, 4096, 1024, 256
LOW, LANE = 640, PIECE // 2
HIGH = WIDTH - LOW
PASSING = 2 * 2**30
VMEM = pl.BlockSpec(memory_space=pltpu.VMEM)
PARAMS = pltpu.CompilerParams(vmem_limit_bytes=40 * 2**20)


def swap_core(a):
    return lax.ppermute(a, C, [(0, 1), (1, 0)])


def swap_y(a, flip):
    return lax.ppermute(a, Y, [(i, i ^ flip) for i in range(4)])


def x_index(place):
    return (place % 2) * 2 + place // 2


def swap_x(a, flip):
    return lax.ppermute(a, (XL, XH), [(x_index(i), x_index(i ^ flip)) for i in range(4)])


def swap_z(a, partners):
    return lax.ppermute(a, Z, list(enumerate(partners)))


NEAR = (1, 0, 3, 2, 5, 4, 7, 6)
NEXT = (7, 2, 1, 4, 3, 6, 5, 0)
FAR = (3, 6, 5, 0, 7, 2, 1, 4)


def slice_of(pos, dxh, dy):
    return ((pos[0] // 2) ^ dxh) * 4 + (pos[1] ^ dy)


def cost(flops, bytes_accessed):
    return pl.CostEstimate(flops=flops, bytes_accessed=bytes_accessed, transcendentals=0)


ANY = pl.BlockSpec(memory_space=pl.ANY)
SCALARS = pl.BlockSpec(memory_space=pltpu.SMEM)


def pick_body(pos, src, out, sems):
    copies = [
        pltpu.make_async_copy(
            src.at[:, pl.ds(pl.multiple_of((2 * j + 1 - pos[2]) * PIECE, PIECE), PIECE)],
            out.at[:, j * PIECE : (j + 1) * PIECE],
            sems.at[j],
        )
        for j in range(8)
    ]
    for copy in copies:
        copy.start()
    for copy in copies:
        copy.wait()


def other_half(pos, tokens):
    return pl.pallas_call(
        pick_body,
        out_shape=jax.ShapeDtypeStruct((ROWS, DEPTH // 2), BF16),
        in_specs=[SCALARS, ANY],
        out_specs=ANY,
        scratch_shapes=[pltpu.SemaphoreType.DMA((8,))],
        compiler_params=PARAMS,
        cost_estimate=cost(0, 2**21),
    )(pos, tokens)


def scaled_pieces(pos, flips, tok, tok_other, in_scale, left):
    y_at = pos[1] ^ pl.program_id(0)
    for n, k in enumerate(flips):
        x_at = pos[0] ^ k
        place = (x_at // 2) * 4 + y_at
        wide = pl.ds(pl.multiple_of(((place * 2 + pos[2]) * 2 + x_at % 2) * LANE, LANE), LANE)
        narrow = pl.ds(pl.multiple_of((place * 2 + x_at % 2) * LANE, LANE), LANE)
        scale = in_scale[:, wide]
        left[:ROWS, n * LANE : (n + 1) * LANE] = (tok[:, wide].astype(F32) * scale).astype(BF16)
        left[ROWS:, n * LANE : (n + 1) * LANE] = (tok_other[:, narrow].astype(F32) * scale).astype(BF16)


def product(left, grad):
    return lax.dot_general(left, grad, (((0,), (0,)), ((), ())), preferred_element_type=F32).astype(BF16)


def first_body(pos, tok, tok_other, in_scale, cot, cot_other, out_scale, grad_ref, one, three, left):
    @pl.when(pl.program_id(0) == 0)
    def _():
        grad_ref[:ROWS] = (cot[...].astype(F32) * out_scale[...]).astype(BF16)
        grad_ref[ROWS:] = (cot_other[...].astype(F32) * out_scale[...]).astype(BF16)

    scaled_pieces(pos, (2, 3), tok, tok_other, in_scale, left)
    one[0] = product(left[:, :LANE], grad_ref[:, :LOW])
    part = product(left[...], grad_ref[:, LOW:])
    three[0, :, :HIGH] = part[:LANE]
    three[0, :, HIGH:] = part[LANE:]


def rest_body(pos, tok, tok_other, in_scale, grad_ref, stay, early_one, late_one, late_three, left):
    scaled_pieces(pos, (0, 1, 3), tok, tok_other, in_scale, left)
    part = product(left[:, : 2 * LANE], grad_ref[...])
    stay[0] = part[:LANE]
    early_one[0] = part[LANE:, :LOW]
    late_one[0] = part[LANE:, LOW:]
    late_three[0] = product(left[:, 2 * LANE :], grad_ref[:, :LOW])


def partials(body, pieces, columns, pos, tokens, tok_other, in_scale, grads):
    whole = lambda shape: pl.BlockSpec(shape, lambda i, pos: (0,) * len(shape))
    out_shape = [jax.ShapeDtypeStruct((4, LANE, n), BF16) for n in columns]
    out_specs = [pl.BlockSpec((1, LANE, n), lambda i, pos: (i, 0, 0)) for n in columns]
    if len(grads) > 1:
        out_shape = [jax.ShapeDtypeStruct((2 * ROWS, WIDTH), BF16)] + out_shape
        out_specs = [whole((2 * ROWS, WIDTH))] + out_specs
    return pl.pallas_call(
        body,
        out_shape=out_shape,
        grid_spec=pltpu.PrefetchScalarGridSpec(
            num_scalar_prefetch=1,
            grid=(4,),
            in_specs=[whole((ROWS, DEPTH)), whole((ROWS, DEPTH // 2)), whole((1, DEPTH))]
            + [whole(g.shape) for g in grads],
            out_specs=out_specs,
            scratch_shapes=[pltpu.VMEM((2 * ROWS, pieces * LANE), BF16)],
        ),
        compiler_params=PARAMS,
        cost_estimate=cost(2 * ROWS * DEPTH // 2 * WIDTH, 5 * 2**20),
    )(pos, tokens, tok_other, in_scale, *grads)


def add_body(late, passing, out):
    out[...] = (late[...].astype(F32) + passing[:, :, : out.shape[2]].astype(F32)).astype(BF16)


def add_passing(late, passing):
    return pl.pallas_call(
        add_body,
        out_shape=jax.ShapeDtypeStruct(late.shape, BF16),
        in_specs=[VMEM] * 2,
        out_specs=VMEM,
        compiler_params=PARAMS,
        cost_estimate=cost(PASSING, 3 * 2**20),
    )(late, passing)


def sum_body(own, early_one, three, late_one, late_three, keep, s1, s2, s3):
    low, high = slice(0, LOW), slice(LOW, WIDTH)
    for k, out in enumerate((keep, s1, s2, s3)):
        for at, early, late in ((low, early_one[k], late_three[k]), (high, three[k, :, HIGH:], late_one[k])):
            total = own[k, :, at].astype(F32) + early.astype(F32) + late.astype(F32)
            out[:, at] = total.astype(out.dtype)


def sum_blocks(own, arrived):
    shape = own.shape[1:]
    return pl.pallas_call(
        sum_body,
        out_shape=[jax.ShapeDtypeStruct(shape, F32)] + [jax.ShapeDtypeStruct(shape, BF16)] * 3,
        in_specs=[VMEM] * 5,
        out_specs=[VMEM] * 4,
        compiler_params=PARAMS,
        cost_estimate=cost(2**20, 4 * 2**20),
    )(own, *arrived)


def join_body(pos, own, r1, r2, r3, keep, send):
    count = LANE // 2
    mine = pos[3]
    for out, at in ((keep, mine), (send, 1 - mine)):
        rows = pl.ds(pl.multiple_of(at * count, count), count)
        total = own[rows]
        for ref in (r1, r2, r3):
            total = total + ref[rows].astype(F32)
        out[...] = total.astype(out.dtype)


def join(pos, own, arrived):
    shape = (LANE // 2, WIDTH)
    return pl.pallas_call(
        join_body,
        out_shape=[jax.ShapeDtypeStruct(shape, F32), jax.ShapeDtypeStruct(shape, BF16)],
        in_specs=[SCALARS] + [VMEM] * 4,
        out_specs=[VMEM] * 2,
        compiler_params=PARAMS,
        cost_estimate=cost(2**20, 2**21),
    )(pos, own, *arrived)


def place_body(scale, pos, own, by_z, by_x, by_both, out):
    count = LANE // 2
    me = (pos[0] % 2) * 2 + pos[3]
    for flip, ref in enumerate((own, by_z, by_x, by_both)):
        at = me ^ flip
        out[pl.ds(pl.multiple_of(at * count, count), count)] = ref[...].astype(F32) * scale


def place(pos, blocks, scale):
    return pl.pallas_call(
        functools.partial(place_body, scale),
        out_shape=jax.ShapeDtypeStruct((PIECE, WIDTH), F32),
        in_specs=[SCALARS] + [VMEM] * 4,
        out_specs=VMEM,
        compiler_params=PARAMS,
        cost_estimate=cost(2**18, 2**20),
    )(pos, *blocks)


def layer_body(order, first, last, pos, tok, tok_other, grad, in_scale, cot, cot_other, *refs):
    count = len(order)
    weights, refs = refs[:count], refs[count:]
    if not first:
        (pre_in, small_in), refs = refs[:2], refs[4:]
    own_ref, other_ref, small = refs[:3]
    if last:
        pre_ref, pre_other, total = refs[3:]
    else:
        (total,) = refs[3:]
    i = pl.program_id(0)

    @pl.when(i == 0)
    def _():
        if first:
            small[...] = jnp.zeros_like(small)
        else:
            total[...] = pre_in[...]
            small[...] = small_in[...]

    for m, (dxh, dy) in enumerate(order):
        @pl.when(i == m)
        def _():
            at = slice_of(pos, dxh, dy)
            wide = pl.ds(pl.multiple_of((at * 2 + pos[2]) * PIECE, PIECE), PIECE)
            narrow = pl.ds(pl.multiple_of(at * PIECE, PIECE), PIECE)
            scale = in_scale[:, wide]
            weight = weights[m][...]
            sums = jnp.zeros((1, PIECE), F32)
            for part, values in ((0, tok[:, wide]), (1, tok_other[:, narrow])):
                rows = slice(part * ROWS, (part + 1) * ROWS)
                values = values.astype(F32)
                scaled = (values * scale).astype(BF16)
                pre = jnp.dot(scaled, weight, preferred_element_type=F32)
                if m == 0 and first:
                    total[rows] = pre
                else:
                    total[rows] += pre
                back = lax.dot_general(
                    grad[rows], weight, (((1,), (1,)), ((), ())), preferred_element_type=F32
                )
                (own_ref, other_ref)[part][...] = (back * scale).astype(BF16)
                sums = sums + jnp.sum(values * back, axis=0, keepdims=True)
            place = at * 2 + pos[2]
            lane = pl.ds(pl.multiple_of((place % 4) * PIECE, PIECE), PIECE)
            small[pl.ds(place // 4, 1), lane] = sums

    if last:
        @pl.when(i == count - 1)
        def _():
            pre_ref[...] = total[:ROWS]
            pre_other[...] = total[ROWS:].astype(BF16)
            small[4:5] = jnp.sum(
                cot[...].astype(F32) * total[:ROWS] + cot_other[...].astype(F32) * total[ROWS:],
                axis=0, keepdims=True,
            )


def layer(pos, orders, step, tokens, tok_other, grad, in_scale, cot, cot_other, weights, before=()):
    whole = lambda shape: pl.BlockSpec(shape, lambda i, pos: (0,) * len(shape))
    shaped = jax.ShapeDtypeStruct
    order, first, last = orders[step], step == 0, step == len(orders) - 1
    start = sum(map(len, orders[:step]))

    def column(i, pos):
        dxh, dy = order[-1]
        for m, flips in enumerate(order[:-1]):
            dxh = jnp.where(i == m, flips[0], dxh)
            dy = jnp.where(i == m, flips[1], dy)
        return 0, slice_of(pos, dxh, dy) * 2 + pos[2]

    both, half = (2 * ROWS, WIDTH), (ROWS, WIDTH)
    small = (8, WIDTH)
    in_specs = [
        whole((ROWS, DEPTH)), whole((ROWS, DEPTH // 2)), whole(both), whole((1, DEPTH)), whole(half), whole(half),
    ] + [whole((PIECE, WIDTH))] * len(order)
    operands = [tokens, tok_other, grad, in_scale, cot, cot_other, *weights]
    aliases = {}
    if not first:
        own, others, sums, pre = before
        aliases = {len(operands) + 3: 0, len(operands) + 4: 1}
        operands += [pre, sums, own, others]
        in_specs += [whole(both), whole(small), ANY, ANY]
    out_shape = [shaped((ROWS, DEPTH), BF16), shaped((ROWS, DEPTH // 2), BF16), shaped(small, F32)]
    out_specs = [
        pl.BlockSpec((ROWS, PIECE), column),
        pl.BlockSpec((ROWS, PIECE), lambda i, pos: (0, i + start)),
        whole(small),
    ]
    if last:
        out_shape += [shaped(half, F32), shaped(half, BF16)]
        out_specs += [whole(half), whole(half)]
    else:
        out_shape += [shaped(both, F32)]
        out_specs += [whole(both)]
    return pl.pallas_call(
        functools.partial(layer_body, order, first, last),
        out_shape=out_shape,
        grid_spec=pltpu.PrefetchScalarGridSpec(
            num_scalar_prefetch=1, grid=(len(order),), in_specs=in_specs, out_specs=out_specs,
            scratch_shapes=[pltpu.VMEM(both, F32)] if last else [],
        ),
        input_output_aliases=aliases,
        compiler_params=PARAMS,
        cost_estimate=cost(1, 1),
    )(pos, *operands)


def fill_body(flips, pos, src, _, out, sems):
    copies = []
    for m, (dxh, dy) in enumerate(flips):
        at = (slice_of(pos, dxh, dy) * 2 + 1 - pos[2]) * PIECE
        copies.append(pltpu.make_async_copy(
            src.at[:, m * PIECE : (m + 1) * PIECE],
            out.at[:, pl.ds(pl.multiple_of(at, PIECE), PIECE)],
            sems.at[m],
        ))
    for copy in copies:
        copy.start()
    for copy in copies:
        copy.wait()


def fill(pos, flips, others, own):
    return pl.pallas_call(
        functools.partial(fill_body, flips),
        out_shape=jax.ShapeDtypeStruct((ROWS, DEPTH), BF16),
        in_specs=[SCALARS, ANY, ANY],
        out_specs=ANY,
        scratch_shapes=[pltpu.SemaphoreType.DMA((8,))],
        input_output_aliases={2: 0},
        compiler_params=PARAMS,
        cost_estimate=cost(0, 2**21),
    )(pos, others, own)


def finish_body(scale, small, in_ref, out_ref):
    total = small[...] * scale
    for k in range(4):
        in_ref[:, k * WIDTH : (k + 1) * WIDTH] = total[k : k + 1]
    out_ref[...] = total[4:5]


def finish(small, scale):
    return pl.pallas_call(
        functools.partial(finish_body, scale),
        out_shape=[jax.ShapeDtypeStruct((1, DEPTH), F32), jax.ShapeDtypeStruct((1, WIDTH), F32)],
        in_specs=[VMEM],
        out_specs=[VMEM] * 2,
        compiler_params=PARAMS,
        cost_estimate=cost(2**14, 2**16),
    )(small)


def on_device(tokens, cotangent, slow_weight, in_scale, out_scale):
    xl, z, xh, y, c = (lax.axis_index(a) for a in (XL, Z, XH, Y, C))
    pos = jnp.stack([2 * xh + xl, y, c, (z ^ (z // 2)) % 2]).astype(jnp.int32)
    member_norm = 1.0 / float(ROWS * 16) ** 0.5
    total_norm = 1.0 / float(ROWS * 256) ** 0.5

    cot_other = swap_core(cotangent)
    one, three = swap_y(slow_weight, 1), swap_y(slow_weight, 3)
    far = swap_x(slow_weight, 3)
    tok_other = swap_core(other_half(pos, tokens))
    grad, by_one, by_three = partials(
        first_body, 2, (LOW, 2 * HIGH), pos, tokens, tok_other, in_scale, (cotangent, cot_other, out_scale)
    )
    by_one, by_three = swap_x(by_one, 1), swap_x(by_three, 3)
    stay, early_one, late_one, late_three = partials(
        rest_body, 3, (WIDTH, LOW, HIGH, LOW), pos, tokens, tok_other, in_scale, (grad,)
    )
    early_one = swap_x(early_one, 1)
    far, one, three, grad, stay = lax.optimization_barrier((far, one, three, grad, stay))

    half = PIECE // 2
    far_one = swap_y(jnp.concatenate([far, three[:half]], axis=0), 1)
    far_three = swap_y(jnp.concatenate([far, one[half:]], axis=0), 3)
    orders = ((0, 0), (0, 1), (0, 3), (1, 0)), ((0, 2), (1, 1), (1, 3)), ((1, 2),)
    run = functools.partial(layer, pos, orders)
    common = (tokens, tok_other, grad, in_scale, cotangent, cot_other)
    state = run(0, *common, (slow_weight, one, three, far))
    late_three = add_passing(late_three, by_one)
    late_one = add_passing(late_one, by_three)
    arrived = [early_one, by_three, swap_x(late_one, 1), swap_x(late_three, 3)]
    far_one, far_three, state, _ = lax.optimization_barrier((far_one, far_three, state, late_one))

    far_two = [swap_y(far_three[:half], 1), swap_y(far_one[half:PIECE], 3)]
    two = jnp.concatenate([far_one[PIECE:], far_three[PIECE:]], axis=0)
    state = run(1, *common, (two, far_one[:PIECE], far_three[:PIECE]), state)
    far_two, state = lax.optimization_barrier((far_two, state))
    arrived, _ = lax.optimization_barrier((arrived, state[3]))
    state = run(2, *common, (jnp.concatenate(far_two, axis=0),), state)
    own, others, small, pre_own, pre_other = state

    stay, *out = sum_blocks(stay, arrived)
    two = swap_y(out[1], 2)
    arrived = [two, swap_y(out[0], 1), swap_y(out[2], 3)]
    small = small + swap_core(small)
    small = small + swap_y(small, 1)
    arrived, small = lax.optimization_barrier((arrived, small))

    keep, out = join(pos, stay, arrived)
    out = swap_z(out, NEAR)
    small = small + swap_y(small, 3)
    out, small = lax.optimization_barrier((out, small))
    mine = (keep + out.astype(F32)).astype(BF16)
    out = swap_z(mine, NEXT)
    small = small + swap_x(small, 2)
    pre_other, others = swap_core(pre_other), swap_core(others)
    mine = (mine.astype(F32) + out.astype(F32)).astype(BF16)
    out = swap_z(mine, FAR)
    result = ((pre_own + pre_other.astype(F32)) * out_scale).astype(BF16)
    grad_tokens = fill(pos, sum(orders, ()), others, own)
    scale_grads = finish(small, member_norm)
    out, scale_grads, result, grad_tokens = lax.optimization_barrier((out, scale_grads, result, grad_tokens))
    mine = (mine.astype(F32) + out.astype(F32)).astype(BF16)
    by_z, by_x = swap_z(mine, NEAR), swap_x(mine, 1)
    by_both = lax.ppermute(mine, (XL, Z), [(i, i ^ 9) for i in range(16)])
    grad_weight = place(pos, (mine, by_z, by_x, by_both), total_norm)
    return result, grad_tokens, grad_weight, *scale_grads


def solution(mesh):
    wide = Mesh(mesh.devices.reshape(2, 8, 2, 4, 2), (XL, Z, XH, Y, C))
    row, member, shard = P((XL, Z, XH, Y, C), None), P((XL, Z), None), P((XH, Y, C), None)
    return jax.shard_map(
        on_device,
        mesh=wide,
        in_specs=(row, row, shard, member, member),
        out_specs=(row, row, shard, member, member),
        check_vma=False,
    )
```

```python
import functools

import jax
import jax.numpy as jnp
from jax import lax
from jax.experimental import pallas as pl
from jax.experimental.pallas import tpu as pltpu
from jax.sharding import Mesh, PartitionSpec as P

F32, BF16 = jnp.float32, jnp.bfloat16
XL, Z, XH, Y, C = "xl", "z", "xh", "y", "c"
ROWS, DEPTH, WIDTH, PIECE = 256, 4096, 1024, 256
LOW, LANE = 640, PIECE // 2
HIGH = WIDTH - LOW
PASSING = 2 * 2**30
VMEM = pl.BlockSpec(memory_space=pltpu.VMEM)
PARAMS = pltpu.CompilerParams(vmem_limit_bytes=40 * 2**20)


def swap_core(a):
    return lax.ppermute(a, C, [(0, 1), (1, 0)])


def swap_y(a, flip):
    return lax.ppermute(a, Y, [(i, i ^ flip) for i in range(4)])


def x_index(place):
    return (place % 2) * 2 + place // 2


def swap_x(a, flip):
    return lax.ppermute(a, (XL, XH), [(x_index(i), x_index(i ^ flip)) for i in range(4)])


def swap_z(a, partners):
    return lax.ppermute(a, Z, list(enumerate(partners)))


NEAR = (1, 0, 3, 2, 5, 4, 7, 6)
NEXT = (7, 2, 1, 4, 3, 6, 5, 0)
FAR = (3, 6, 5, 0, 7, 2, 1, 4)


def slice_of(pos, dxh, dy):
    return ((pos[0] // 2) ^ dxh) * 4 + (pos[1] ^ dy)


def cost(flops, bytes_accessed):
    return pl.CostEstimate(flops=flops, bytes_accessed=bytes_accessed, transcendentals=0)


ANY = pl.BlockSpec(memory_space=pl.ANY)
SCALARS = pl.BlockSpec(memory_space=pltpu.SMEM)


def pick_body(pos, src, out, sems):
    copies = [
        pltpu.make_async_copy(
            src.at[:, pl.ds(pl.multiple_of((2 * j + 1 - pos[2]) * PIECE, PIECE), PIECE)],
            out.at[:, j * PIECE : (j + 1) * PIECE],
            sems.at[j],
        )
        for j in range(8)
    ]
    for copy in copies:
        copy.start()
    for copy in copies:
        copy.wait()


def other_half(pos, tokens):
    return pl.pallas_call(
        pick_body,
        out_shape=jax.ShapeDtypeStruct((ROWS, DEPTH // 2), BF16),
        in_specs=[SCALARS, ANY],
        out_specs=ANY,
        scratch_shapes=[pltpu.SemaphoreType.DMA((8,))],
        compiler_params=PARAMS,
        cost_estimate=cost(0, 2**21),
    )(pos, tokens)


def scaled_pieces(pos, flips, tok, tok_other, in_scale, left):
    y_at = pos[1] ^ pl.program_id(0)
    for n, k in enumerate(flips):
        x_at = pos[0] ^ k
        place = (x_at // 2) * 4 + y_at
        wide = pl.ds(pl.multiple_of(((place * 2 + pos[2]) * 2 + x_at % 2) * LANE, LANE), LANE)
        narrow = pl.ds(pl.multiple_of((place * 2 + x_at % 2) * LANE, LANE), LANE)
        scale = in_scale[:, wide]
        left[:ROWS, n * LANE : (n + 1) * LANE] = (tok[:, wide].astype(F32) * scale).astype(BF16)
        left[ROWS:, n * LANE : (n + 1) * LANE] = (tok_other[:, narrow].astype(F32) * scale).astype(BF16)


def product(left, grad):
    return lax.dot_general(left, grad, (((0,), (0,)), ((), ())), preferred_element_type=F32).astype(BF16)


def first_body(pos, tok, tok_other, in_scale, cot, cot_other, out_scale, grad_ref, one, three, left):
    @pl.when(pl.program_id(0) == 0)
    def _():
        grad_ref[:ROWS] = (cot[...].astype(F32) * out_scale[...]).astype(BF16)
        grad_ref[ROWS:] = (cot_other[...].astype(F32) * out_scale[...]).astype(BF16)

    scaled_pieces(pos, (2, 3), tok, tok_other, in_scale, left)
    one[0] = product(left[:, :LANE], grad_ref[:, :LOW])
    part = product(left[...], grad_ref[:, LOW:])
    three[0, :, :HIGH] = part[:LANE]
    three[0, :, HIGH:] = part[LANE:]


def rest_body(pos, tok, tok_other, in_scale, grad_ref, stay, early_one, late_one, late_three, left):
    scaled_pieces(pos, (0, 1, 3), tok, tok_other, in_scale, left)
    part = product(left[:, : 2 * LANE], grad_ref[...])
    stay[0] = part[:LANE]
    early_one[0] = part[LANE:, :LOW]
    late_one[0] = part[LANE:, LOW:]
    late_three[0] = product(left[:, 2 * LANE :], grad_ref[:, :LOW])


def partials(body, pieces, columns, pos, tokens, tok_other, in_scale, grads):
    whole = lambda shape: pl.BlockSpec(shape, lambda i, pos: (0,) * len(shape))
    out_shape = [jax.ShapeDtypeStruct((4, LANE, n), BF16) for n in columns]
    out_specs = [pl.BlockSpec((1, LANE, n), lambda i, pos: (i, 0, 0)) for n in columns]
    if len(grads) > 1:
        out_shape = [jax.ShapeDtypeStruct((2 * ROWS, WIDTH), BF16)] + out_shape
        out_specs = [whole((2 * ROWS, WIDTH))] + out_specs
    return pl.pallas_call(
        body,
        out_shape=out_shape,
        grid_spec=pltpu.PrefetchScalarGridSpec(
            num_scalar_prefetch=1,
            grid=(4,),
            in_specs=[whole((ROWS, DEPTH)), whole((ROWS, DEPTH // 2)), whole((1, DEPTH))]
            + [whole(g.shape) for g in grads],
            out_specs=out_specs,
            scratch_shapes=[pltpu.VMEM((2 * ROWS, pieces * LANE), BF16)],
        ),
        compiler_params=PARAMS,
        cost_estimate=cost(2 * ROWS * DEPTH // 2 * WIDTH, 5 * 2**20),
    )(pos, tokens, tok_other, in_scale, *grads)


def add_body(late, passing, out):
    out[...] = (late[...].astype(F32) + passing[:, :, : out.shape[2]].astype(F32)).astype(BF16)


def add_passing(late, passing):
    return pl.pallas_call(
        add_body,
        out_shape=jax.ShapeDtypeStruct(late.shape, BF16),
        in_specs=[VMEM] * 2,
        out_specs=VMEM,
        compiler_params=PARAMS,
        cost_estimate=cost(PASSING, 3 * 2**20),
    )(late, passing)


def sum_body(own, early_one, three, late_one, late_three, keep, s1, s2, s3):
    low, high = slice(0, LOW), slice(LOW, WIDTH)
    for k, out in enumerate((keep, s1, s2, s3)):
        for at, early, late in ((low, early_one[k], late_three[k]), (high, three[k, :, HIGH:], late_one[k])):
            total = own[k, :, at].astype(F32) + early.astype(F32) + late.astype(F32)
            out[:, at] = total.astype(out.dtype)


def sum_blocks(own, arrived):
    shape = own.shape[1:]
    return pl.pallas_call(
        sum_body,
        out_shape=[jax.ShapeDtypeStruct(shape, F32)] + [jax.ShapeDtypeStruct(shape, BF16)] * 3,
        in_specs=[VMEM] * 5,
        out_specs=[VMEM] * 4,
        compiler_params=PARAMS,
        cost_estimate=cost(2**20, 4 * 2**20),
    )(own, *arrived)


def join_body(pos, own, r1, r2, r3, keep, send):
    count = LANE // 2
    mine = pos[3]
    for out, at in ((keep, mine), (send, 1 - mine)):
        rows = pl.ds(pl.multiple_of(at * count, count), count)
        total = own[rows]
        for ref in (r1, r2, r3):
            total = total + ref[rows].astype(F32)
        out[...] = total.astype(out.dtype)


def join(pos, own, arrived):
    shape = (LANE // 2, WIDTH)
    return pl.pallas_call(
        join_body,
        out_shape=[jax.ShapeDtypeStruct(shape, F32), jax.ShapeDtypeStruct(shape, BF16)],
        in_specs=[SCALARS] + [VMEM] * 4,
        out_specs=[VMEM] * 2,
        compiler_params=PARAMS,
        cost_estimate=cost(2**20, 2**21),
    )(pos, own, *arrived)


def place_body(scale, pos, own, by_z, by_x, by_both, out):
    count = LANE // 2
    me = (pos[0] % 2) * 2 + pos[3]
    for flip, ref in enumerate((own, by_z, by_x, by_both)):
        at = me ^ flip
        out[pl.ds(pl.multiple_of(at * count, count), count)] = ref[...].astype(F32) * scale


def place(pos, blocks, scale):
    return pl.pallas_call(
        functools.partial(place_body, scale),
        out_shape=jax.ShapeDtypeStruct((PIECE, WIDTH), F32),
        in_specs=[SCALARS] + [VMEM] * 4,
        out_specs=VMEM,
        compiler_params=PARAMS,
        cost_estimate=cost(2**18, 2**20),
    )(pos, *blocks)


def layer_body(order, first, last, pos, tok, tok_other, grad, in_scale, cot, cot_other, *refs):
    count = len(order)
    weights, refs = refs[:count], refs[count:]
    if not first:
        (pre_in, small_in), refs = refs[:2], refs[4:]
    own_ref, other_ref, small = refs[:3]
    if last:
        pre_ref, pre_other, total = refs[3:]
    else:
        (total,) = refs[3:]
    i = pl.program_id(0)

    @pl.when(i == 0)
    def _():
        if first:
            small[...] = jnp.zeros_like(small)
        else:
            total[...] = pre_in[...]
            small[...] = small_in[...]

    for m, (dxh, dy) in enumerate(order):
        @pl.when(i == m)
        def _():
            at = slice_of(pos, dxh, dy)
            wide = pl.ds(pl.multiple_of((at * 2 + pos[2]) * PIECE, PIECE), PIECE)
            narrow = pl.ds(pl.multiple_of(at * PIECE, PIECE), PIECE)
            scale = in_scale[:, wide]
            weight = weights[m][...]
            sums = jnp.zeros((1, PIECE), F32)
            for part, values in ((0, tok[:, wide]), (1, tok_other[:, narrow])):
                rows = slice(part * ROWS, (part + 1) * ROWS)
                values = values.astype(F32)
                scaled = (values * scale).astype(BF16)
                pre = jnp.dot(scaled, weight, preferred_element_type=F32)
                if m == 0 and first:
                    total[rows] = pre
                else:
                    total[rows] += pre
                back = lax.dot_general(
                    grad[rows], weight, (((1,), (1,)), ((), ())), preferred_element_type=F32
                )
                (own_ref, other_ref)[part][...] = (back * scale).astype(BF16)
                sums = sums + jnp.sum(values * back, axis=0, keepdims=True)
            place = at * 2 + pos[2]
            lane = pl.ds(pl.multiple_of((place % 4) * PIECE, PIECE), PIECE)
            small[pl.ds(place // 4, 1), lane] = sums

    if last:
        @pl.when(i == count - 1)
        def _():
            pre_ref[...] = total[:ROWS]
            pre_other[...] = total[ROWS:].astype(BF16)
            small[4:5] = jnp.sum(
                cot[...].astype(F32) * total[:ROWS] + cot_other[...].astype(F32) * total[ROWS:],
                axis=0, keepdims=True,
            )


def layer(pos, orders, step, tokens, tok_other, grad, in_scale, cot, cot_other, weights, before=()):
    whole = lambda shape: pl.BlockSpec(shape, lambda i, pos: (0,) * len(shape))
    shaped = jax.ShapeDtypeStruct
    order, first, last = orders[step], step == 0, step == len(orders) - 1
    start = sum(map(len, orders[:step]))

    def column(i, pos):
        dxh, dy = order[-1]
        for m, flips in enumerate(order[:-1]):
            dxh = jnp.where(i == m, flips[0], dxh)
            dy = jnp.where(i == m, flips[1], dy)
        return 0, slice_of(pos, dxh, dy) * 2 + pos[2]

    both, half = (2 * ROWS, WIDTH), (ROWS, WIDTH)
    small = (8, WIDTH)
    in_specs = [
        whole((ROWS, DEPTH)), whole((ROWS, DEPTH // 2)), whole(both), whole((1, DEPTH)), whole(half), whole(half),
    ] + [whole((PIECE, WIDTH))] * len(order)
    operands = [tokens, tok_other, grad, in_scale, cot, cot_other, *weights]
    aliases = {}
    if not first:
        own, others, sums, pre = before
        aliases = {len(operands) + 3: 0, len(operands) + 4: 1}
        operands += [pre, sums, own, others]
        in_specs += [whole(both), whole(small), ANY, ANY]
    out_shape = [shaped((ROWS, DEPTH), BF16), shaped((ROWS, DEPTH // 2), BF16), shaped(small, F32)]
    out_specs = [
        pl.BlockSpec((ROWS, PIECE), column),
        pl.BlockSpec((ROWS, PIECE), lambda i, pos: (0, i + start)),
        whole(small),
    ]
    if last:
        out_shape += [shaped(half, F32), shaped(half, BF16)]
        out_specs += [whole(half), whole(half)]
    else:
        out_shape += [shaped(both, F32)]
        out_specs += [whole(both)]
    return pl.pallas_call(
        functools.partial(layer_body, order, first, last),
        out_shape=out_shape,
        grid_spec=pltpu.PrefetchScalarGridSpec(
            num_scalar_prefetch=1, grid=(len(order),), in_specs=in_specs, out_specs=out_specs,
            scratch_shapes=[pltpu.VMEM(both, F32)] if last else [],
        ),
        input_output_aliases=aliases,
        compiler_params=PARAMS,
        cost_estimate=cost(1, 1),
    )(pos, *operands)


def fill_body(flips, pos, src, _, out, sems):
    copies = []
    for m, (dxh, dy) in enumerate(flips):
        at = (slice_of(pos, dxh, dy) * 2 + 1 - pos[2]) * PIECE
        copies.append(pltpu.make_async_copy(
            src.at[:, m * PIECE : (m + 1) * PIECE],
            out.at[:, pl.ds(pl.multiple_of(at, PIECE), PIECE)],
            sems.at[m],
        ))
    for copy in copies:
        copy.start()
    for copy in copies:
        copy.wait()


def fill(pos, flips, others, own):
    return pl.pallas_call(
        functools.partial(fill_body, flips),
        out_shape=jax.ShapeDtypeStruct((ROWS, DEPTH), BF16),
        in_specs=[SCALARS, ANY, ANY],
        out_specs=ANY,
        scratch_shapes=[pltpu.SemaphoreType.DMA((8,))],
        input_output_aliases={2: 0},
        compiler_params=PARAMS,
        cost_estimate=cost(0, 2**21),
    )(pos, others, own)


def finish_body(scale, small, in_ref, out_ref):
    total = small[...] * scale
    for k in range(4):
        in_ref[:, k * WIDTH : (k + 1) * WIDTH] = total[k : k + 1]
    out_ref[...] = total[4:5]


def finish(small, scale):
    return pl.pallas_call(
        functools.partial(finish_body, scale),
        out_shape=[jax.ShapeDtypeStruct((1, DEPTH), F32), jax.ShapeDtypeStruct((1, WIDTH), F32)],
        in_specs=[VMEM],
        out_specs=[VMEM] * 2,
        compiler_params=PARAMS,
        cost_estimate=cost(2**14, 2**16),
    )(small)


def on_device(tokens, cotangent, slow_weight, in_scale, out_scale):
    xl, z, xh, y, c = (lax.axis_index(a) for a in (XL, Z, XH, Y, C))
    pos = jnp.stack([2 * xh + xl, y, c, (z ^ (z // 2)) % 2]).astype(jnp.int32)
    member_norm = 1.0 / float(ROWS * 16) ** 0.5
    total_norm = 1.0 / float(ROWS * 256) ** 0.5

    cot_other = swap_core(cotangent)
    one, three = swap_y(slow_weight, 1), swap_y(slow_weight, 3)
    far = swap_x(slow_weight, 3)
    tok_other = swap_core(other_half(pos, tokens))
    grad, by_one, by_three = partials(
        first_body, 2, (LOW, 2 * HIGH), pos, tokens, tok_other, in_scale, (cotangent, cot_other, out_scale)
    )
    by_one, by_three = swap_x(by_one, 1), swap_x(by_three, 3)
    stay, early_one, late_one, late_three = partials(
        rest_body, 3, (WIDTH, LOW, HIGH, LOW), pos, tokens, tok_other, in_scale, (grad,)
    )
    early_one = swap_x(early_one, 1)
    far, one, three, grad, stay = lax.optimization_barrier((far, one, three, grad, stay))

    half = PIECE // 2
    far_one = swap_y(jnp.concatenate([far, three[:half]], axis=0), 1)
    far_three = swap_y(jnp.concatenate([far, one[half:]], axis=0), 3)
    orders = ((0, 0), (0, 1), (0, 3), (1, 0)), ((0, 2), (1, 1), (1, 3)), ((1, 2),)
    run = functools.partial(layer, pos, orders)
    common = (tokens, tok_other, grad, in_scale, cotangent, cot_other)
    state = run(0, *common, (slow_weight, one, three, far))
    late_three = add_passing(late_three, by_one)
    late_one = add_passing(late_one, by_three)
    arrived = [early_one, by_three, swap_x(late_one, 1), swap_x(late_three, 3)]
    far_one, far_three, state, _ = lax.optimization_barrier((far_one, far_three, state, late_one))

    far_two = [swap_y(far_three[:half], 1), swap_y(far_one[half:PIECE], 3)]
    two = jnp.concatenate([far_one[PIECE:], far_three[PIECE:]], axis=0)
    state = run(1, *common, (two, far_one[:PIECE], far_three[:PIECE]), state)
    far_two, state = lax.optimization_barrier((far_two, state))
    arrived, _ = lax.optimization_barrier((arrived, state[3]))
    state = run(2, *common, (jnp.concatenate(far_two, axis=0),), state)
    own, others, small, pre_own, pre_other = state

    stay, *out = sum_blocks(stay, arrived)
    arrived = [swap_y(out[0], 1), swap_y(out[2], 3), swap_y(out[1], 2)]
    small = small + swap_core(small)
    small = small + swap_y(small, 1)
    arrived, small = lax.optimization_barrier((arrived, small))

    keep, out = join(pos, stay, arrived)
    out = swap_z(out, NEAR)
    small = small + swap_y(small, 3)
    out, small = lax.optimization_barrier((out, small))
    mine = (keep + out.astype(F32)).astype(BF16)
    out = swap_z(mine, NEXT)
    small = small + swap_x(small, 2)
    pre_other, others = swap_core(pre_other), swap_core(others)
    mine = (mine.astype(F32) + out.astype(F32)).astype(BF16)
    out = swap_z(mine, FAR)
    result = ((pre_own + pre_other.astype(F32)) * out_scale).astype(BF16)
    grad_tokens = fill(pos, sum(orders, ()), others, own)
    scale_grads = finish(small, member_norm)
    out, scale_grads, result, grad_tokens = lax.optimization_barrier((out, scale_grads, result, grad_tokens))
    mine = (mine.astype(F32) + out.astype(F32)).astype(BF16)
    by_z, by_x = swap_z(mine, NEAR), swap_x(mine, 1)
    by_both = lax.ppermute(mine, (XL, Z), [(i, i ^ 9) for i in range(16)])
    grad_weight = place(pos, (mine, by_z, by_x, by_both), total_norm)
    return result, grad_tokens, grad_weight, *scale_grads


def solution(mesh):
    wide = Mesh(mesh.devices.reshape(2, 8, 2, 4, 2), (XL, Z, XH, Y, C))
    row, member, shard = P((XL, Z, XH, Y, C), None), P((XL, Z), None), P((XH, Y, C), None)
    return jax.shard_map(
        on_device,
        mesh=wide,
        in_specs=(row, row, shard, member, member),
        out_specs=(row, row, shard, member, member),
        check_vma=False,
    )
```
